32 devices in a mesh: dp: 16 (over z, y, core), tensor: 2 (over x).
Axes of the slice: x: 2, y: 2, z: 4, core: 2. Of those that a mesh axis runs over, the one named last changes fastest.
Arguments:
- residual_in: bfloat16 [32768, 1024], P(('dp', 'tensor')), may hold values from -6 to 6
- mixer_gain: float32 [1024], replicated, may hold values from 0.1 to 1.9
- in_weight: bfloat16 [1024, 8, 768], P(None, 'tensor'), may hold values from -0.1875 to 0.1875
- rate_weight: bfloat16 [1024, 8, 2], P(None, 'tensor'), may hold values from -0.1875 to 0.1875
- conv_weight: bfloat16 [8, 4, 512], P('tensor'), may hold values from -3 to 3
- decay_log: float32 [8], P('tensor'), may hold values from -1.5 to 2
- decay_bias: float32 [8], P('tensor'), may hold values from -7 to -2
- head_gain: float32 [256], replicated, may hold values from 0.1 to 1.9
- out_weight: bfloat16 [8, 256, 1024], P('tensor'), may hold values from -0.25 to 0.25
- ffn_gain: float32 [1024], replicated, may hold values from 0.1 to 1.9
- gate_up: bfloat16 [1024, 2, 2816], P(None, None, 'tensor'), may hold values from -0.1875 to 0.1875
- down_weight: bfloat16 [2816, 1024], P('tensor'), may hold values from -0.109375 to 0.109375
- segments: int32 [32768], P('dp'), may hold values from 0 to 2, as said below
- pad_mask: int32 [32768], P('dp'), may hold values from 0 to 1, as said below
- out_grad: bfloat16 [32768, 1024], P(('dp', 'tensor')), may hold values from -6 to 6
Outputs:
- layer_out: bfloat16 [32768, 1024], P(('dp', 'tensor'))
- input_grad: bfloat16 [32768, 1024], P(('dp', 'tensor'))
- grad_mixer_gain: float32 [1024], replicated
- grad_in_weight: float32 [1024, 8, 768], P(None, 'tensor')
- grad_rate_weight: float32 [1024, 8, 2], P(None, 'tensor')
- grad_conv_weight: float32 [8, 4, 512], P('tensor')
- grad_decay_log: float32 [8], P('tensor')
- grad_decay_bias: float32 [8], P('tensor')
- grad_head_gain: float32 [256], replicated
- grad_out_weight: float32 [8, 256, 1024], P('tensor')
- grad_ffn_gain: float32 [1024], replicated
- grad_gate_up: float32 [1024, 2, 2816], P(None, None, 'tensor')
- grad_down_weight: float32 [2816, 1024], P('tensor')
The draws below stay inside these ranges and needn't reach their ends.
Inputs may be any that keep to these rules, and one draw needn't show every extreme that they name: `segments`: in each aligned run of 1024 tokens (one sequence) the numbers start at 0, never fall and name three documents of 200 tokens or more; the last is followed by 1 to 128 padding tokens that carry its number. `pad_mask`: 0 exactly on the padding tokens at the end of each sequence, 1 elsewhere.
All inputs are finite; a program needn't handle non-finite values.
Results may differ from the reference program's by a relative error of at most 0.024.
Values may be sent and summed in bfloat16 or wider, within the bound.
No kernel may reach another device: no remote copies, remote signals or barrier semaphores. Data moves between devices by JAX's collectives and lax.ppermute only.
A program may use at most 512 MiB of HBM per device.

```python
import jax
import jax.numpy as jnp
from jax import lax

D = 1024
H = 8
DK = 128
DV = 256
FF = 2816
CONV = 4
SPAN = 64
SEQ = 1024
DOC_MIN = 200
PAD_MOST = 128
TOK_DEV = 2048
TOKENS = 32768


def doc_layout(key):
    count = TOKENS // SEQ
    pad_key, first_key, second_key = jax.random.split(key, 3)
    pad_len = jax.random.randint(pad_key, (count,), 1, PAD_MOST + 1)
    usable = SEQ - pad_len
    cut_one = jax.random.randint(first_key, (count,), DOC_MIN, usable - 2 * DOC_MIN + 1)
    cut_two = jax.random.randint(second_key, (count,), cut_one + DOC_MIN, usable - DOC_MIN + 1)
    places = jnp.arange(SEQ, dtype=jnp.int32)[None, :]
    seg_ids = (places >= cut_one[:, None]).astype(jnp.int32) + (places >= cut_two[:, None]).astype(jnp.int32)
    keep_mask = (places < usable[:, None]).astype(jnp.int32)
    return (seg_ids.reshape(-1), keep_mask.reshape(-1))


def draw_segments(key, part):
    return doc_layout(key)[0]


def draw_pad_mask(key, part):
    return doc_layout(key)[1]


def steps_of(stream_key, shape, shards, smallest, largest):
    gain, own = 1.0, jax.random.fold_in(stream_key, 6)
    for position, shards_of in shards:
        steps = jnp.exp(jax.random.uniform(jax.random.fold_in(own, position), (shards_of,), jnp.float32, smallest / len(shards), largest / len(shards)))
        gain = gain * jnp.repeat(steps, shape[position] // shards_of).reshape([-1 if axis == position else 1 for axis in range(len(shape))])
    return gain


def noise(key, dims, deviation, bound, shards=(), kind=jnp.bfloat16):
    entries = deviation * jax.random.normal(key, dims, jnp.float32)
    if shards:
        entries = entries * steps_of(key, dims, shards, -0.22, 0.18)
    return jnp.clip(entries, -bound, bound).astype(kind)


def setup_inputs(seed: int = 0) -> dict:
    keys = jax.random.split(jax.random.key(seed), 16)
    residual_in = noise(keys[0], (TOKENS, D), 1.0, 6.0, ((0, 32),))
    mixer_gain = jnp.clip(1.0 + 0.18 * jax.random.normal(keys[1], (D,), jnp.float32), 0.1, 1.9)
    in_weight = noise(keys[2], (D, H, 2 * DK + 2 * DV), D ** -0.5, 0.1875, ((1, 2),))
    rate_weight = noise(keys[3], (D, H, 2), D ** -0.5, 0.1875, ((1, 2),))
    conv_weight = noise(keys[4], (H, CONV, 2 * DK + DV), 0.5, 3.0, ((0, 2),))
    decay_log = jnp.clip(-1.5 + 3.5 * jax.random.uniform(keys[5], (H,), jnp.float32) ** steps_of(keys[5], (H,), ((0, 2),), -0.2, 0.2), -1.5, 2.0)
    decay_bias = jnp.clip(-7.0 + 5.0 * jax.random.uniform(keys[6], (H,), jnp.float32) ** steps_of(keys[6], (H,), ((0, 2),), -0.2, 0.2), -7.0, -2.0)
    head_gain = jnp.clip(1.0 + 0.18 * jax.random.normal(keys[7], (DV,), jnp.float32), 0.1, 1.9)
    out_weight = noise(keys[8], (H, DV, D), (H * DV // 4) ** -0.5, 0.25, ((0, 2),))
    ffn_gain = jnp.clip(1.0 + 0.18 * jax.random.normal(keys[9], (D,), jnp.float32), 0.1, 1.9)
    gate_up = noise(keys[10], (D, 2, FF), D ** -0.5, 0.1875, ((2, 2),))
    down_weight = noise(keys[11], (FF, D), FF ** -0.5, 0.109375, ((0, 2),))
    segments = draw_segments(jax.random.fold_in(keys[15], 71), 0)
    pad_mask = draw_pad_mask(jax.random.fold_in(keys[15], 71), 0)
    out_grad = noise(keys[14], (TOKENS, D), 1.0, 6.0, ((0, 32),))
    return dict(residual_in=residual_in, mixer_gain=mixer_gain, in_weight=in_weight, rate_weight=rate_weight, conv_weight=conv_weight, decay_log=decay_log, decay_bias=decay_bias, head_gain=head_gain, out_weight=out_weight, ffn_gain=ffn_gain, gate_up=gate_up, down_weight=down_weight, segments=segments, pad_mask=pad_mask, out_grad=out_grad)


@jax.custom_vjp
def low(v):
    return lax.optimization_barrier(v.astype(jnp.bfloat16)).astype(jnp.float32)

@jax.custom_vjp
def low_back(v):
    return v

def low_keep(v):
    return (low(v), None)

def low_pass(kept, grad):
    return (grad,)

def back_keep(v):
    return (v, None)

def back_low(kept, grad):
    return (low(grad),)
low.defvjp(low_keep, low_pass)
low_back.defvjp(back_keep, back_low)

def rms_norm(rows_in, gain_in):
    return rows_in * lax.rsqrt(lax.optimization_barrier(jnp.mean(rows_in * rows_in, -1, keepdims=True)) + 1e-05) * gain_in

def short_conv(pre_conv, seg_rows, conv_in):
    summed = pre_conv * conv_in[:, 0, :]
    for offset in range(1, conv_in.shape[1]):
        shifted = jnp.pad(pre_conv, ((0, 0), (offset, 0), (0, 0), (0, 0)))[:, :-offset]
        seg_shift = jnp.pad(seg_rows, ((0, 0), (offset, 0)), constant_values=-1)[:, :-offset]
        usable = (seg_shift == seg_rows).astype(jnp.float32)
        summed = summed + shifted * usable[:, :, None, None] * conv_in[:, offset, :]
    return jax.nn.silu(summed)

def span_step(carry, block):
    current_state, last_seg = carry
    query_rows, key_vector, values_vec, write_rate, log_decay, seg_ids, keep_mask = block
    width = seg_ids.shape[0]
    cum_decay = jnp.cumsum(log_decay, axis=1)
    carry_on = (seg_ids == last_seg).astype(jnp.float32)
    same_seg = seg_ids[:, None] == seg_ids[None, :]
    lower_eq = jnp.tril(jnp.ones((width, width), dtype=bool))
    lower_strict = jnp.tril(jnp.ones((width, width), dtype=bool), -1)
    inside = same_seg & lower_eq
    gap_decay = cum_decay[:, :, None] - cum_decay[:, None, :]
    weight_eq = jnp.where(inside, jnp.exp(jnp.where(inside, gap_decay, 0.0)), 0.0)
    weight_strict = weight_eq * lower_strict.astype(jnp.float32)
    key_key = jnp.einsum('htk,hsk->hts', key_vector, key_vector, precision=lax.Precision.HIGHEST)
    system = write_rate[:, :, None] * weight_strict * key_key
    initial_scale = jnp.exp(cum_decay) * carry_on[None, :]
    key_from_state = jnp.einsum('afy,aym->afm', key_vector, current_state, precision=lax.Precision.HIGHEST)
    right_side = write_rate[:, :, None] * (values_vec - initial_scale[:, :, None] * key_from_state)
    written_value = lax.linalg.triangular_solve(system, right_side, left_side=True, lower=True, unit_diagonal=True)
    query_key = jnp.einsum('htk,hsk->hts', query_rows, key_vector, precision=lax.Precision.HIGHEST) * weight_eq
    query_from_state = jnp.einsum('afy,aym->afm', query_rows, current_state, precision=lax.Precision.HIGHEST)
    outputs = jnp.einsum('hts,hsv->htv', query_key, written_value, precision=lax.Precision.HIGHEST)
    outputs = (outputs + initial_scale[:, :, None] * query_from_state) * keep_mask[None, :, None]
    final_weight = weight_eq[:, -1, :]
    updated_state = initial_scale[:, -1][:, None, None] * current_state + jnp.einsum('au,aul,aup->alp', final_weight, key_vector, written_value, precision=lax.Precision.HIGHEST)
    return ((updated_state, seg_ids[-1]), outputs)

def run_sequence(query_rows, key_vector, values_vec, write_rate, log_decay, seg_blocks, mask_blocks):
    initial = (jnp.zeros((query_rows.shape[1], query_rows.shape[3], values_vec.shape[3]), jnp.float32), jnp.full((), -1, jnp.int32))
    unused_state, outputs = lax.scan(jax.checkpoint(span_step), initial, (query_rows, key_vector, values_vec, write_rate, log_decay, seg_blocks, mask_blocks))
    return outputs

def mixer_core(projected, rate_pre, conv_in, log_in, bias_in, gain_in, seg_in, mask_in, seq_len, span_len):
    length, heads, in_width = projected.shape
    value_dim = gain_in.shape[0]
    mix_width = conv_in.shape[2]
    key_dim = (mix_width - value_dim) // 2
    seq_count = length // seq_len
    span_count = seq_len // span_len
    pre_conv = projected[:, :, :mix_width].reshape(seq_count, seq_len, heads, mix_width)
    seg_rows = seg_in.reshape(seq_count, seq_len)
    mask_rows = mask_in.reshape(seq_count, seq_len).astype(jnp.float32)
    mixed = short_conv(pre_conv, seg_rows, conv_in)
    query_rows = mixed[..., :key_dim]
    key_vector = mixed[..., key_dim:2 * key_dim]
    values_vec = mixed[..., 2 * key_dim:]
    query_rows = query_rows * lax.rsqrt(lax.optimization_barrier(jnp.sum(query_rows * query_rows, -1, keepdims=True)) + 1e-06) * key_dim ** (-0.5)
    key_vector = key_vector * lax.rsqrt(lax.optimization_barrier(jnp.sum(key_vector * key_vector, -1, keepdims=True)) + 1e-06)
    write_rate = jax.nn.sigmoid(rate_pre[..., 1]).reshape(seq_count, seq_len, heads) * mask_rows[:, :, None]
    log_decay = -jnp.exp(log_in) * jax.nn.softplus(rate_pre[..., 0].reshape(seq_count, seq_len, heads) + bias_in)

    def wide_blocks(array):
        return array.reshape(seq_count, span_count, span_len, heads, -1).transpose(0, 1, 3, 2, 4)

    def flat_blocks(array):
        return array.reshape(seq_count, span_count, span_len, heads).transpose(0, 1, 3, 2)
    outputs = jax.vmap(run_sequence)(wide_blocks(query_rows), wide_blocks(key_vector), wide_blocks(values_vec), flat_blocks(write_rate), flat_blocks(log_decay), seg_rows.reshape(seq_count, span_count, span_len), mask_rows.reshape(seq_count, span_count, span_len))
    heads_out = outputs.transpose(0, 1, 3, 2, 4).reshape(length, heads, value_dim)
    gate_part = projected[:, :, mix_width:]
    normed = heads_out * lax.rsqrt(lax.optimization_barrier(jnp.mean(heads_out * heads_out, -1, keepdims=True)) + 1e-05) * gain_in
    return (normed * jax.nn.silu(gate_part)).reshape(length, heads * value_dim)

def reference(residual_in, mixer_gain, in_weight, rate_weight, conv_weight, decay_log, decay_bias, head_gain, out_weight, ffn_gain, gate_up, down_weight, segments, pad_mask, out_grad):
    floats = tuple((item.astype(jnp.float32) for item in (residual_in, mixer_gain, in_weight, rate_weight, conv_weight, decay_log, decay_bias, head_gain, out_weight, ffn_gain, gate_up, down_weight)))

    def forward(rows_all, gain_one, w_in, w_rate, w_conv, log_in, bias_in, gain_head, w_out, gain_two, w_gu, w_down):

        def one_group(group):
            rows, seg_group, mask_group = group
            first_low = low(rms_norm(rows, gain_one))
            projected = low_back(jnp.dot(first_low, w_in.reshape(D, -1), precision=lax.Precision.HIGHEST))
            projected = projected.reshape(-1, H, 2 * DK + 2 * DV)
            rate_pre = low_back(jnp.dot(first_low, w_rate.reshape(D, -1), precision=lax.Precision.HIGHEST))
            rate_pre = rate_pre.reshape(-1, H, 2)
            gated = low(mixer_core(projected, rate_pre, w_conv, log_in, bias_in, gain_head, seg_group, mask_group, SEQ, SPAN))
            mixer_out = low_back(jnp.dot(gated, w_out.reshape(H * DV, D), precision=lax.Precision.HIGHEST))
            middle = rows + mixer_out
            second = low(rms_norm(middle, gain_two))
            pre_ffn = low_back(jnp.dot(second, w_gu.reshape(D, 2 * FF), precision=lax.Precision.HIGHEST))
            pre_ffn = pre_ffn.reshape(-1, 2, FF)
            hidden = low(jax.nn.silu(pre_ffn[:, 0]) * pre_ffn[:, 1])
            return middle + low_back(jnp.dot(hidden, w_down, precision=lax.Precision.HIGHEST))
        groups = TOKENS // TOK_DEV
        result = lax.map(jax.checkpoint(one_group), (rows_all.reshape(groups, TOK_DEV, D), segments.reshape(groups, TOK_DEV), pad_mask.reshape(groups, TOK_DEV)))
        return result.reshape(TOKENS, D)
    layer_out, pullback = jax.vjp(forward, *floats)
    grads = pullback(out_grad.astype(jnp.float32))
    return (layer_out.astype(jnp.bfloat16), grads[0].astype(jnp.bfloat16), grads[1], grads[2], grads[3], grads[4], grads[5], grads[6], grads[7], grads[8], grads[9], grads[10], grads[11])
```

```python
import functools

import jax
import jax.numpy as jnp
from jax import lax
from jax.experimental import pallas as pl
from jax.experimental.pallas import tpu as pltpu
from jax.sharding import PartitionSpec as P

SEQ = 1024
BLOCK = 256
PART = 512
HALO = 16
F32 = jnp.float32
BF16 = jnp.bfloat16
VMEM_BYTES = 56 * 1024 * 1024


def dot_nn(left, right):
    return lax.dot_general(left, right, (((1,), (0,)), ((), ())), preferred_element_type=F32)


def dot_nt(left, right):
    return lax.dot_general(left, right, (((1,), (1,)), ((), ())), preferred_element_type=F32)


def dot_tn(left, right):
    return lax.dot_general(left, right, (((0,), (0,)), ((), ())), preferred_element_type=F32)


def sigmoid(values):
    return 0.5 * jnp.tanh(0.5 * values) + 0.5


def row_sum(values):
    return jnp.sum(values, axis=1, keepdims=True)


MASK, BACK, AHEAD, SEGMENT, PER_HEAD = 0, 1, 4, 7, 8
WRITE, CUM, START, LAST = 0, 1, 2, 3


def fill_level_masks(mask_ref):
    levels, width, unused_width = mask_ref.shape
    later = lax.broadcasted_iota(jnp.int32, (width, width), 0)
    earlier = lax.broadcasted_iota(jnp.int32, (width, width), 1)
    apart = later ^ earlier
    for level in range(levels):
        chosen = (later > earlier) & ((apart >> level) == 1)
        mask_ref[level] = jnp.where(chosen, 1.0, 0.0).astype(BF16)


def unit_lower_inverses(systems, mask_ref):
    width = systems[0].shape[0]
    identity = jnp.where(
        lax.broadcasted_iota(jnp.int32, (width, width), 0)
        == lax.broadcasted_iota(jnp.int32, (width, width), 1),
        1.0,
        0.0,
    ).astype(BF16)
    inverses = [identity - system * mask_ref[0] for system in systems]
    level = 1
    while (2 << level) <= width:
        size = 1 << level
        if size < 16:
            halves = [dot_nn(inv, system).astype(BF16) for inv, system in zip(inverses, systems)]
            joined = [dot_nn(half, inv).astype(BF16) for half, inv in zip(halves, inverses)]
            inverses = [inv - both * mask_ref[level] for inv, both in zip(inverses, joined)]
        elif (2 << level) < width:
            starts = range(size, width, 2 * size)
            odd = [
                jnp.concatenate([inv[at : at + size] for at in starts], axis=0) for inv in inverses
            ]
            halves = [dot_nn(rows, system).astype(BF16) for rows, system in zip(odd, systems)]
            joined = [dot_nn(half, inv).astype(BF16) for half, inv in zip(halves, inverses)]
            chosen = jnp.concatenate([mask_ref[level, at : at + size, :] for at in starts], axis=0)
            odd = [rows - both * chosen for rows, both in zip(odd, joined)]
            inverses = [
                jnp.concatenate(
                    [
                        part
                        for place, at in enumerate(starts)
                        for part in (
                            inv[at - size : at],
                            rows[place * size : (place + 1) * size],
                        )
                    ],
                    axis=0,
                )
                for inv, rows in zip(inverses, odd)
            ]
        else:
            halves = [
                dot_nn(inv[size:, size:], system[size:, :size]).astype(BF16)
                for inv, system in zip(inverses, systems)
            ]
            joined = [
                dot_nn(half, inv[:size, :size]).astype(BF16) for half, inv in zip(halves, inverses)
            ]
            inverses = [
                jnp.concatenate(
                    [inv[:size], jnp.concatenate([-both, inv[size:, size:]], axis=1)], axis=0
                )
                for inv, both in zip(inverses, joined)
            ]
        level += 1
    return inverses


def conv_rows(padded_ref, head, cols, conv_ref):
    width = cols.shape[0]
    taps = conv_ref.shape[1]
    shifted = [padded_ref[head, HALO : HALO + width, :]]
    for offset in range(1, taps):
        usable = cols[:, BACK + offset - 1 : BACK + offset]
        shifted.append(padded_ref[head, HALO - offset : HALO - offset + width, :] * usable)
    summed = shifted[0] * conv_ref[head, 0:1, :]
    for offset in range(1, taps):
        summed = summed + shifted[offset] * conv_ref[head, offset : offset + 1, :]
    return summed, shifted


def gap_offsets(cols, rows):
    width = cols.shape[0]
    later = lax.broadcasted_iota(jnp.int32, (width, width), 0)
    earlier = lax.broadcasted_iota(jnp.int32, (width, width), 1)
    inside = (cols[:, SEGMENT : SEGMENT + 1] == rows[0:1, :]) & (later >= earlier)
    return jnp.where(inside, 0.0, -1e30)


def head_column(cols, head, which):
    place = PER_HEAD + 4 * head + which
    return cols[:, place : place + 1]


def fill_halo(padded_ref, head, at, before_ref, halo_ref, first):
    mix_width = padded_ref.shape[2]

    @pl.when(first)
    def _():
        padded_ref[head, 0:HALO, :] = before_ref[:, at : at + mix_width].astype(F32)

    @pl.when(jnp.logical_not(first))
    def _():
        padded_ref[head, 0:HALO, :] = halo_ref[:, at : at + mix_width].astype(F32)


def fwd_kernel(
    proj_ref, halo_ref, before_ref, cols_ref, rows_ref, conv_ref, gain_ref, initial_ref,
    gated_ref, out_ref, written_ref, inverse_ref, start_ref, state_ref,
    padded_ref, mask_ref,
):
    heads, taps, mix_width = conv_ref.shape
    value_dim = gain_ref.shape[1]
    key_dim = (mix_width - value_dim) // 2
    in_width = mix_width + value_dim
    width = proj_ref.shape[0]
    block = pl.program_id(0)

    @pl.when(block == 0)
    def _():
        fill_level_masks(mask_ref)
        state_ref[...] = initial_ref[...]

    for h in range(heads):
        fill_halo(padded_ref, h, h * in_width, before_ref, halo_ref, block == 0)

    cols = cols_ref[...]
    rows = rows_ref[...]
    offsets = gap_offsets(cols, rows)
    every = range(heads)
    queries, keys, values = [], [], []
    for h in every:
        at = h * in_width
        padded_ref[h, HALO : HALO + width, :] = proj_ref[:, at : at + mix_width].astype(F32)
        summed, unused_rows = conv_rows(padded_ref, h, cols, conv_ref)
        mixed = summed * sigmoid(summed)
        query = mixed[:, :key_dim]
        key = mixed[:, key_dim : 2 * key_dim]
        query = query * (lax.rsqrt(row_sum(query * query) + 1e-06) * key_dim ** (-0.5))
        key = key * lax.rsqrt(row_sum(key * key) + 1e-06)
        queries.append(query.astype(BF16))
        keys.append(key)
        values.append(mixed[:, 2 * key_dim :])
    keys_low = [key.astype(BF16) for key in keys]
    stacked = [jnp.concatenate([k, q], axis=0) for k, q in zip(keys_low, queries)]
    products = [dot_nt(both, key) for both, key in zip(stacked, keys_low)]
    weights = [
        jnp.exp(head_column(cols, h, CUM) - rows[1 + h : 2 + h, :] + offsets) for h in every
    ]
    systems = [
        (products[h][:width] * weights[h] * head_column(cols, h, WRITE)).astype(BF16)
        for h in every
    ]
    reads = [(products[h][width:] * weights[h]).astype(BF16) for h in every]
    inverses = unit_lower_inverses(systems, mask_ref)
    states = [state_ref[h] for h in every]
    states_low = [state.astype(BF16) for state in states]
    from_state = [dot_nn(both, state) for both, state in zip(stacked, states_low)]
    right = [
        (
            head_column(cols, h, WRITE)
            * (values[h] - head_column(cols, h, START) * from_state[h][:width])
        ).astype(BF16)
        for h in every
    ]
    written = [dot_nn(inv, side).astype(BF16) for inv, side in zip(inverses, right)]
    inner = [dot_nn(read, value) for read, value in zip(reads, written)]
    added = [
        dot_tn((keys[h] * head_column(cols, h, LAST)).astype(BF16), written[h]) for h in every
    ]
    keep = cols[:, MASK : MASK + 1]
    for h in every:
        start_ref[0, h] = states_low[h]
        inverse_ref[0, h] = inverses[h]
        written_ref[:, h * value_dim : (h + 1) * value_dim] = written[h]
        final = head_column(cols, h, START)[width - 1 : width, :]
        state_ref[h] = final * states[h] + added[h]
        out = (inner[h] + head_column(cols, h, START) * from_state[h][width:]) * keep
        out_ref[:, h * value_dim : (h + 1) * value_dim] = out.astype(BF16)
        scale = lax.rsqrt(row_sum(out * out) * (1.0 / value_dim) + 1e-05)
        at = h * in_width + mix_width
        gate = proj_ref[:, at : at + value_dim].astype(F32)
        gated = out * scale * gain_ref[...] * (gate * sigmoid(gate))
        gated_ref[:, h * value_dim : (h + 1) * value_dim] = gated.astype(BF16)


def bwd_kernel(
    cot_ref, proj_ref, halo_ref, before_ref, cols_ref, rows_ref, conv_ref, gain_ref,
    out_ref, written_ref, inverse_ref, start_ref, initial_ref, after_ref,
    grad_ref, tokens_ref, colsum_ref, conv_grad_ref, gain_grad_ref, state_ref, stash_ref,
    padded_ref, ahead_ref,
):
    heads, taps, mix_width = conv_ref.shape
    value_dim = gain_ref.shape[1]
    key_dim = (mix_width - value_dim) // 2
    in_width = mix_width + value_dim
    width = proj_ref.shape[0]
    step = pl.program_id(0)

    @pl.when(step == 0)
    def _():
        conv_grad_ref[...] = jnp.zeros_like(conv_grad_ref)
        gain_grad_ref[...] = jnp.zeros_like(gain_grad_ref)
        state_ref[...] = initial_ref[...]
        ahead_ref[:, width : width + HALO, :] = after_ref[...]

    for h in range(heads):
        fill_halo(
            padded_ref, h, h * in_width, before_ref, halo_ref, step == pl.num_programs(0) - 1
        )

    cols = cols_ref[...]
    rows = rows_ref[...]
    offsets = gap_offsets(cols, rows)
    every = range(heads)
    keep = cols[:, MASK : MASK + 1]
    strict = (
        lax.broadcasted_iota(jnp.int32, (width, width), 0)
        > lax.broadcasted_iota(jnp.int32, (width, width), 1)
    )

    cots, gain_grad = [], jnp.zeros((1, value_dim), F32)
    for h in every:
        at = h * in_width + mix_width
        cot = cot_ref[:, h * value_dim : (h + 1) * value_dim].astype(F32)
        out = out_ref[:, h * value_dim : (h + 1) * value_dim].astype(F32)
        gate = proj_ref[:, at : at + value_dim].astype(F32)
        scale = lax.rsqrt(row_sum(out * out) * (1.0 / value_dim) + 1e-05)
        gate_sig = sigmoid(gate)
        normed = out * scale
        through = cot * gate * gate_sig
        gain_grad = gain_grad + jnp.sum(through * normed, axis=0, keepdims=True)
        grad_normed = through * gain_ref[...]
        mean = row_sum(grad_normed * normed) * (1.0 / value_dim)
        cots.append((scale * (grad_normed - normed * mean) * keep))
        grad_gate = cot * normed * gain_ref[...] * gate_sig * (1.0 + gate * (1.0 - gate_sig))
        grad_ref[:, at : at + value_dim] = grad_gate.astype(BF16)
    gain_grad_ref[...] += gain_grad

    queries, keys = [], []
    for h in every:
        at = h * in_width
        padded_ref[h, HALO : HALO + width, :] = proj_ref[:, at : at + mix_width].astype(F32)
        summed, unused_rows = conv_rows(padded_ref, h, cols, conv_ref)
        qk = summed[:, : 2 * key_dim]
        mixed = qk * sigmoid(qk)
        query = mixed[:, :key_dim]
        key = mixed[:, key_dim:]
        query = query * (lax.rsqrt(row_sum(query * query) + 1e-06) * key_dim ** (-0.5))
        key = key * lax.rsqrt(row_sum(key * key) + 1e-06)
        queries.append(query)
        keys.append(key)
        ahead_ref[h, 0:width, :] = summed
    keys_low = [key.astype(BF16) for key in keys]
    queries_low = [query.astype(BF16) for query in queries]
    products = [
        dot_nt(jnp.concatenate([k, q], axis=0), k) for k, q in zip(keys_low, queries_low)
    ]
    weights = [
        jnp.exp(head_column(cols, h, CUM) - rows[1 + h : 2 + h, :] + offsets) for h in every
    ]
    cots_low = [cot.astype(BF16) for cot in cots]
    grad_states = [state_ref[h] for h in every]
    grad_states_low = [state.astype(BF16) for state in grad_states]
    written = [written_ref[:, h * value_dim : (h + 1) * value_dim] for h in every]
    reads = [(products[h][width:] * weights[h]).astype(BF16) for h in every]
    last_keys = [keys[h] * head_column(cols, h, LAST) for h in every]
    grad_written = [
        (
            dot_tn(reads[h], cots_low[h]) + dot_nn(last_keys[h].astype(BF16), grad_states_low[h])
        ).astype(BF16)
        for h in every
    ]
    grad_right = [dot_tn(inverse_ref[0, h], grad_written[h]) for h in every]
    grad_values = [grad_right[h] * head_column(cols, h, WRITE) for h in every]
    against = [
        dot_nt(jnp.concatenate([cots_low[h], grad_right[h].astype(BF16)], axis=0), written[h])
        for h in every
    ]
    grad_reads = [against[h][:width] * weights[h] for h in every]
    grad_pairs = [
        jnp.where(strict, against[h][width:] * weights[h], 0.0) * -head_column(cols, h, WRITE)
        for h in every
    ]
    gaps = [
        grad_reads[h] * products[h][width:] + grad_pairs[h] * products[h][:width] for h in every
    ]
    starts = [
        jnp.concatenate(
            [
                (cots[h] * head_column(cols, h, START)).astype(BF16),
                (grad_values[h] * -head_column(cols, h, START)).astype(BF16),
            ],
            axis=0,
        )
        for h in every
    ]
    both_grads = [
        jnp.concatenate([grad_reads[h].astype(BF16), grad_pairs[h].astype(BF16)], axis=0)
        for h in every
    ]
    by_key = [dot_nn(both_grads[h], keys_low[h]) for h in every]
    by_state = [dot_nt(starts[h], start_ref[0, h]) for h in every]
    both_rows = [
        jnp.concatenate([queries_low[h], keys_low[h]], axis=0) for h in every
    ]
    turned = [dot_tn(both_grads[h], both_rows[h]) for h in every]
    by_last = [dot_nt(written[h], grad_states_low[h]) for h in every]
    states_part = [dot_tn(both_rows[h], starts[h]) for h in every]

    lane = lax.broadcasted_iota(jnp.int32, tokens_ref.shape, 1)
    place = lax.broadcasted_iota(jnp.int32, (width, 1), 0)
    packed = jnp.zeros(tokens_ref.shape, F32)
    for h in every:
        from_state = by_state[h]
        grad_query = by_key[h][:width] + from_state[:width]
        grad_key = (
            by_key[h][width:]
            + from_state[width:]
            + turned[h]
            + by_last[h] * head_column(cols, h, LAST)
        )
        log_last = row_sum(by_last[h] * last_keys[h])
        log_start = row_sum(queries[h] * from_state[:width] + keys[h] * from_state[width:])
        final = head_column(cols, h, START)[width - 1 : width, :]
        start_f32 = start_ref[0, h].astype(F32)
        total = jnp.sum(log_last, axis=0, keepdims=True) + final * jnp.sum(
            row_sum(start_f32 * grad_states[h]), axis=0, keepdims=True
        )
        grad_cum = row_sum(gaps[h]) + log_start - log_last + jnp.where(
            place == width - 1, total, 0.0
        )
        grad_logit = row_sum(grad_right[h] * written[h].astype(F32))
        packed = packed + jnp.where(lane == 2 * h, grad_cum, 0.0)
        packed = packed + jnp.where(lane == 2 * h + 1, grad_logit, 0.0)
        colsum_ref[h : h + 1, :] = jnp.sum(gaps[h], axis=0, keepdims=True)
        state_ref[h] = final * grad_states[h] + states_part[h]

        summed = ahead_ref[h, 0:width, :]
        sig = sigmoid(summed)
        slope = sig * (1.0 + summed * (1.0 - sig))
        mixed = summed[:, : 2 * key_dim] * sig[:, : 2 * key_dim]
        query = mixed[:, :key_dim]
        key = mixed[:, key_dim:]
        query_scale = lax.rsqrt(row_sum(query * query) + 1e-06)
        key_scale = lax.rsqrt(row_sum(key * key) + 1e-06)
        grad_query = grad_query * key_dim ** (-0.5)
        query_unit = query * query_scale
        key_unit = key * key_scale
        grad_query = query_scale * (grad_query - query_unit * row_sum(grad_query * query_unit))
        grad_key = key_scale * (grad_key - key_unit * row_sum(grad_key * key_unit))
        ahead_ref[h, 0:width, 0:key_dim] = grad_query * slope[:, :key_dim]
        ahead_ref[h, 0:width, key_dim : 2 * key_dim] = (
            grad_key * slope[:, key_dim : 2 * key_dim]
        )
        ahead_ref[h, 0:width, 2 * key_dim :] = grad_values[h] * slope[:, 2 * key_dim :]
        grad_summed = ahead_ref[h, 0:width, :]
        at = h * in_width
        grad_pre = grad_summed * conv_ref[h, 0:1, :]
        conv_grad_ref[h, 0:1, :] += jnp.sum(
            grad_summed * padded_ref[h, HALO : HALO + width, :], axis=0, keepdims=True
        )
        for offset in range(1, taps):
            usable = cols[:, AHEAD + offset - 1 : AHEAD + offset]
            later = ahead_ref[h, offset : offset + width, :] * usable
            grad_pre = grad_pre + later * conv_ref[h, offset : offset + 1, :]
            back = cols[:, BACK + offset - 1 : BACK + offset]
            earlier = padded_ref[h, HALO - offset : HALO - offset + width, :] * back
            conv_grad_ref[h, offset : offset + 1, :] += jnp.sum(
                grad_summed * earlier, axis=0, keepdims=True
            )
        grad_ref[:, at : at + mix_width] = grad_pre.astype(BF16)
        ahead_ref[h, width : width + HALO, :] = ahead_ref[h, 0:HALO, :]
        stash_ref[h] = ahead_ref[h, 0:HALO, :]
    tokens_ref[...] = packed


def segment_tables(segments, pad_mask, width):
    length = segments.shape[0]
    place = jnp.arange(length, dtype=jnp.int32)

    def moved(array, by):
        if by > 0:
            return jnp.concatenate([jnp.full((by,), -1, array.dtype), array[:-by]])
        return jnp.concatenate([array[-by:], jnp.full((-by,), -1, array.dtype)])

    back = [
        ((moved(segments, by) == segments) & (place >= by)).astype(F32) for by in (1, 2, 3)
    ]
    ahead = [
        ((moved(segments, -by) == segments) & (place + by < length)).astype(F32)
        for by in (1, 2, 3)
    ]
    seg_blocks = segments.reshape(-1, width)
    ends = seg_blocks[:, -1]
    carried = (seg_blocks == moved(ends, 1)[:, None]).astype(F32).reshape(-1)
    to_last = (seg_blocks == ends[:, None]).astype(F32).reshape(-1)
    return jnp.stack(
        [pad_mask.astype(F32), *back, *ahead, segments.astype(F32), carried, to_last]
    )


def token_tables(rate_rows, table, decay_log, decay_bias, width):
    heads, length = rate_rows.shape[1:]
    write = jax.nn.sigmoid(rate_rows[1]) * table[0]
    log_decay = -jnp.exp(decay_log)[:, None] * jax.nn.softplus(
        rate_rows[0] + decay_bias[:, None]
    )
    upper = jnp.triu(jnp.ones((width, width), F32))
    cum = jnp.dot(
        log_decay.reshape(-1, width), upper, precision=lax.Precision.HIGHEST
    ).reshape(heads, length)
    cum_blocks = cum.reshape(heads, -1, width)
    start = jnp.exp(cum) * table[8]
    last = jnp.exp(cum_blocks[:, :, -1:] - cum_blocks).reshape(heads, length) * table[9]
    per_head = jnp.stack([write, cum, start, last], axis=1).reshape(4 * heads, length)
    cols = jnp.concatenate([table[:8], per_head]).T
    rows = jnp.concatenate(
        [table[7:8], cum, jnp.zeros((-(1 + heads) % 8, length), F32)], axis=0
    )
    return cols, rows, log_decay


def whole_block(array):
    return pl.BlockSpec(array.shape, lambda c: (0,) * array.ndim)


def mixer_forward(proj, before, cols, rows, conv, gain, initial, width):
    heads, taps, mix_width = conv.shape
    value_dim = gain.shape[1]
    key_dim = (mix_width - value_dim) // 2
    length = proj.shape[0]
    steps = length // width

    def here(c):
        return (c, 0)

    def halo(c):
        return (jnp.maximum(c * (width // HALO) - 1, 0), 0)

    levels = width.bit_length() - 1
    wide = pl.BlockSpec((width, heads * value_dim), here)
    wide_shape = jax.ShapeDtypeStruct((length, heads * value_dim), BF16)
    return pl.pallas_call(
        fwd_kernel,
        grid=(steps,),
        in_specs=[
            pl.BlockSpec((width, proj.shape[1]), here),
            pl.BlockSpec((HALO, proj.shape[1]), halo),
            whole_block(before),
            pl.BlockSpec((width, cols.shape[1]), here),
            pl.BlockSpec((rows.shape[0], width), lambda c: (0, c)),
            whole_block(conv),
            whole_block(gain),
            whole_block(initial),
        ],
        out_specs=[
            wide,
            wide,
            wide,
            pl.BlockSpec((1, heads, width, width), lambda c: (c, 0, 0, 0)),
            pl.BlockSpec((1, heads, key_dim, value_dim), lambda c: (c, 0, 0, 0)),
            whole_block(initial),
        ],
        out_shape=[
            wide_shape,
            wide_shape,
            wide_shape,
            jax.ShapeDtypeStruct((steps, heads, width, width), BF16),
            jax.ShapeDtypeStruct((steps, heads, key_dim, value_dim), BF16),
            jax.ShapeDtypeStruct(initial.shape, F32),
        ],
        scratch_shapes=[
            pltpu.VMEM((heads, HALO + width, mix_width), F32),
            pltpu.VMEM((levels, width, width), BF16),
        ],
        compiler_params=pltpu.CompilerParams(vmem_limit_bytes=VMEM_BYTES),
        cost_estimate=pl.CostEstimate(
            flops=heads * steps * 16 * width * width * value_dim,
            bytes_accessed=6 * length * heads * in_total(conv, gain),
            transcendentals=0,
        ),
        name="mixer_forward",
    )(proj, proj, before, cols, rows, conv, gain, initial)


def in_total(conv, gain):
    return conv.shape[2] + gain.shape[1]


def mixer_backward(cot, proj, before, cols, rows, conv, gain, kept, initial, after, width):
    out, written, inverse, start = kept
    heads, taps, mix_width = conv.shape
    value_dim = gain.shape[1]
    key_dim = (mix_width - value_dim) // 2
    length = proj.shape[0]
    steps = length // width

    def at(c):
        return steps - 1 - c

    def here(c):
        return (at(c), 0)

    def halo(c):
        return (jnp.maximum(at(c) * (width // HALO) - 1, 0), 0)

    wide = pl.BlockSpec((width, heads * value_dim), here)
    sums = -(-heads // 8) * 8
    return pl.pallas_call(
        bwd_kernel,
        grid=(steps,),
        in_specs=[
            wide,
            pl.BlockSpec((width, proj.shape[1]), here),
            pl.BlockSpec((HALO, proj.shape[1]), halo),
            whole_block(before),
            pl.BlockSpec((width, cols.shape[1]), here),
            pl.BlockSpec((rows.shape[0], width), lambda c: (0, at(c))),
            whole_block(conv),
            whole_block(gain),
            wide,
            wide,
            pl.BlockSpec((1, heads, width, width), lambda c: (at(c), 0, 0, 0)),
            pl.BlockSpec((1, heads, key_dim, value_dim), lambda c: (at(c), 0, 0, 0)),
            whole_block(initial),
            whole_block(after),
        ],
        out_specs=[
            pl.BlockSpec((width, proj.shape[1]), here),
            pl.BlockSpec((width, 2 * heads), here),
            pl.BlockSpec((sums, width), lambda c: (0, at(c))),
            whole_block(conv),
            whole_block(gain),
            whole_block(initial),
            whole_block(after),
        ],
        out_shape=[
            jax.ShapeDtypeStruct(proj.shape, BF16),
            jax.ShapeDtypeStruct((length, 2 * heads), F32),
            jax.ShapeDtypeStruct((sums, length), F32),
            jax.ShapeDtypeStruct(conv.shape, F32),
            jax.ShapeDtypeStruct(gain.shape, F32),
            jax.ShapeDtypeStruct(initial.shape, F32),
            jax.ShapeDtypeStruct(after.shape, F32),
        ],
        scratch_shapes=[
            pltpu.VMEM((heads, HALO + width, mix_width), F32),
            pltpu.VMEM((heads, width + HALO, mix_width), F32),
        ],
        compiler_params=pltpu.CompilerParams(vmem_limit_bytes=VMEM_BYTES),
        cost_estimate=pl.CostEstimate(
            flops=heads * steps * 16 * width * width * value_dim,
            bytes_accessed=8 * length * heads * in_total(conv, gain),
            transcendentals=0,
        ),
        name="mixer_backward",
    )(cot, proj, proj, before, cols, rows, conv, gain, out, written, inverse, start, initial, after)


def rate_gradients(tokens, colsum, rate_rows, mask_row, decay_log, decay_bias, log_decay, width):
    heads, length = log_decay.shape
    turned = tokens.T.reshape(heads, 2, length)
    grad_cum = turned[:, 0] - colsum[:heads]
    lower = jnp.tril(jnp.ones((width, width), F32))
    grad_log_decay = jnp.dot(
        grad_cum.reshape(-1, width), lower, precision=lax.Precision.HIGHEST
    ).reshape(heads, length)
    shifted = rate_rows[0] + decay_bias[:, None]
    grad_decay = grad_log_decay * -jnp.exp(decay_log)[:, None] * jax.nn.sigmoid(shifted)
    grad_write = turned[:, 1] * (1.0 - jax.nn.sigmoid(rate_rows[1])) * mask_row
    return (
        jnp.stack([grad_decay, grad_write]),
        jnp.sum(grad_log_decay * log_decay, axis=1),
        jnp.sum(grad_decay, axis=1),
    )


def ffn_kernel(
    second_ref, second_turned_ref, cot_ref, cot_turned_ref, gate_ref, up_ref, down_ref,
    sum_ref, back_ref, grads_ref,
):
    shares, unused_kinds, rows, tile = grads_ref.shape

    @pl.when(pl.program_id(0) == 0)
    def _():
        sum_ref[...] = jnp.zeros_like(sum_ref)
        back_ref[...] = jnp.zeros_like(back_ref)

    gate = dot_nn(second_ref[...], gate_ref[...])
    up = dot_nn(second_ref[...], up_ref[...])
    grad_hidden = dot_nn(cot_ref[...], down_ref[...])
    sig = sigmoid(gate)
    active = gate * sig
    hidden = (active * up).astype(BF16)
    grad_up = (grad_hidden * active).astype(BF16)
    grad_gate = (grad_hidden * up * sig * (1.0 + gate * (1.0 - sig))).astype(BF16)
    sum_ref[...] += dot_nt(hidden, down_ref[...])
    back_ref[...] += dot_nt(grad_gate, gate_ref[...]) + dot_nt(grad_up, up_ref[...])
    for kind, (turned_ref, right) in enumerate(
        ((second_turned_ref, grad_gate), (second_turned_ref, grad_up), (cot_turned_ref, hidden))
    ):
        grads_ref[:, kind] = (
            dot_nn(turned_ref[...], right).astype(BF16).reshape(shares, rows, tile)
        )


def feed_forward(second, second_turned, cot, weights, shares):
    length, model_width = second.shape
    hidden = weights.shape[1] // 3
    tile = 256
    tiles = hidden // tile
    square = jax.ShapeDtypeStruct((length, model_width), F32)
    rows = model_width // shares

    def third(kind):
        return pl.BlockSpec((model_width, tile), lambda j: (0, kind * tiles + j))

    turned = (second_turned, cot.T)
    return pl.pallas_call(
        ffn_kernel,
        grid=(tiles,),
        in_specs=[
            whole_block(second),
            whole_block(turned[0]),
            whole_block(cot),
            whole_block(turned[1]),
            third(0),
            third(1),
            third(2),
        ],
        out_specs=[
            whole_block(square),
            whole_block(square),
            pl.BlockSpec((shares, 3, rows, tile), lambda j: (0, 0, 0, j)),
        ],
        out_shape=[square, square, jax.ShapeDtypeStruct((shares, 3, rows, hidden), BF16)],
        compiler_params=pltpu.CompilerParams(vmem_limit_bytes=VMEM_BYTES),
        cost_estimate=pl.CostEstimate(
            flops=6 * length * model_width * hidden,
            bytes_accessed=12 * model_width * hidden,
            transcendentals=0,
        ),
        name="feed_forward",
    )(second, turned[0], cot, turned[1], weights, weights, weights)


def in_grad_kernel(count, *refs):
    low_refs, refs, grad_ref, turned_ref = (
        refs[:count], refs[count : 2 * count], refs[-2], refs[-1]
    )
    size = refs[0].shape[0]

    @pl.when(pl.program_id(0) == 0)
    def _():
        for place, ref in enumerate(low_refs):
            turned_ref[:, place * size : (place + 1) * size] = (
                ref[...].astype(F32).T.astype(BF16)
            )

    total = dot_nn(turned_ref[:, 0:size], refs[0][...])
    for place, ref in enumerate(refs[1:], 1):
        total = total + dot_nn(turned_ref[:, place * size : (place + 1) * size], ref[...])
    grad_ref[...] = total.astype(BF16)


def in_grad(lows, parts, tile):
    size, model_width = lows[0].shape
    columns = parts[0].shape[1]
    return pl.pallas_call(
        functools.partial(in_grad_kernel, len(parts)),
        grid=(columns // tile,),
        in_specs=[whole_block(low) for low in lows]
        + [pl.BlockSpec((size, tile), lambda j: (0, j)) for unused in parts],
        out_specs=pl.BlockSpec((model_width, tile), lambda j: (0, j)),
        out_shape=jax.ShapeDtypeStruct((model_width, columns), BF16),
        scratch_shapes=[pltpu.VMEM((model_width, size * len(parts)), BF16)],
        compiler_params=pltpu.CompilerParams(vmem_limit_bytes=VMEM_BYTES),
        cost_estimate=pl.CostEstimate(
            flops=2 * model_width * size * columns,
            bytes_accessed=2 * model_width * columns,
            transcendentals=0,
        ),
        name="in_grad",
    )(*lows, *parts)


ROWS = 256


def norm_kernel(rows_ref, gain_ref, low_ref):
    rows = rows_ref[...].astype(F32)
    scale = lax.rsqrt(row_sum(rows * rows) * (1.0 / rows.shape[1]) + 1e-05)
    low_ref[...] = (rows * scale * gain_ref[...]).astype(BF16)


def part_specs(parts):
    specs, starts, start = [], [], 0
    for part in parts:
        blocks = part.shape[0] // ROWS
        specs.append(
            pl.BlockSpec(
                (ROWS, part.shape[1]),
                lambda i, start=start, blocks=blocks: (jnp.clip(i - start, 0, blocks - 1), 0),
            )
        )
        starts.append(start)
        start += blocks
    return specs, starts


def gathered_rows(part_refs, starts, total_ref):
    block = pl.program_id(0)
    for refs, start, end in zip(part_refs, starts, starts[1:] + [1 << 30]):

        @pl.when((block >= start) & (block < end))
        def _(refs=refs):
            total = refs[0][...].astype(F32)
            for ref in refs[1:]:
                total = total + ref[...].astype(F32)
            total_ref[...] = total

    return total_ref[...]


def middle_kernel(starts, per_part, rows_ref, gain_ref, *refs):
    part_refs = refs[: len(starts) * per_part]
    middle_ref, second_ref, turned_ref, total_ref = refs[len(part_refs) :]
    grouped = [part_refs[at : at + per_part] for at in range(0, len(part_refs), per_part)]
    middle = rows_ref[...].astype(F32) + gathered_rows(grouped, starts, total_ref)
    scale = lax.rsqrt(row_sum(middle * middle) * (1.0 / middle.shape[1]) + 1e-05)
    second = middle * scale * gain_ref[...]
    middle_ref[...] = middle
    second_ref[...] = second.astype(BF16)
    turned_ref[...] = second.T.astype(BF16)


def norm_back(rows, gain, grad):
    width = rows.shape[1]
    scale = lax.rsqrt(row_sum(rows * rows) * (1.0 / width) + 1e-05)
    unit = rows * scale
    through = grad * gain
    grad_rows = scale * (through - unit * (row_sum(through * unit) * (1.0 / width)))
    return grad_rows, jnp.sum(grad * unit, axis=0, keepdims=True)


def add_rows(total_ref, row):
    @pl.when(pl.program_id(0) == 0)
    def _():
        total_ref[...] = jnp.zeros_like(total_ref)

    total_ref[...] += row


def second_back_kernel(
    back_ref, middle_ref, cot_ref, sum_ref, gain_ref, out_ref, grad_ref, low_ref, gain_grad_ref
):
    middle = middle_ref[...]
    out_ref[...] = (middle + sum_ref[...]).astype(BF16)
    grad_rows, gain_grad = norm_back(middle, gain_ref[...], back_ref[...])
    add_rows(gain_grad_ref, gain_grad)
    grad_middle = cot_ref[...].astype(F32) + grad_rows
    grad_ref[...] = grad_middle
    low_ref[...] = grad_middle.astype(BF16)


def first_back_kernel(starts, per_part, rows_ref, middle_grad_ref, gain_ref, *refs):
    part_refs = refs[: len(starts) * per_part]
    grad_ref, gain_grad_ref, total_ref = refs[len(part_refs) :]
    grouped = [part_refs[at : at + per_part] for at in range(0, len(part_refs), per_part)]
    grad = gathered_rows(grouped, starts, total_ref)
    grad_rows, gain_grad = norm_back(rows_ref[...].astype(F32), gain_ref[...], grad)
    add_rows(gain_grad_ref, gain_grad)
    grad_ref[...] = (middle_grad_ref[...] + grad_rows).astype(BF16)


def row_call(kernel, rows, operands, outs, scratch, name):
    width = rows[1]
    block = pl.BlockSpec((ROWS, width), lambda i: (i, 0))
    kinds = {
        "rows": (block, (rows[0], width)),
        "turned": (pl.BlockSpec((width, ROWS), lambda i: (0, i)), (width, rows[0])),
        "gain": (pl.BlockSpec((1, width), lambda i: (0, 0)), (1, width)),
    }
    return pl.pallas_call(
        kernel,
        grid=(rows[0] // ROWS,),
        in_specs=[block if spec is None else spec for unused, spec in operands],
        out_specs=[kinds[kind][0] for kind, unused in outs],
        out_shape=[jax.ShapeDtypeStruct(kinds[kind][1], dtype) for kind, dtype in outs],
        scratch_shapes=scratch,
        compiler_params=pltpu.CompilerParams(vmem_limit_bytes=VMEM_BYTES),
        name=name,
    )(*[array for array, unused in operands])


def norm_rows(rows, gain):
    gain = gain[None]
    return row_call(
        norm_kernel, rows.shape, [(rows, None), (gain, whole_block(gain))], [("rows", BF16)], [], "norm_rows"
    )[0]


def middle_rows(rows, gain, parts):
    gain = gain[None]
    specs, starts = part_specs([terms[0] for terms in parts])
    operands = [(rows, None), (gain, whole_block(gain))]
    for terms, spec in zip(parts, specs):
        operands += [(term, spec) for term in terms]
    return row_call(
        functools.partial(middle_kernel, starts, len(parts[0])),
        rows.shape,
        operands,
        [("rows", F32), ("rows", BF16), ("turned", BF16)],
        [pltpu.VMEM((ROWS, rows.shape[1]), F32)],
        "middle_rows",
    )


def second_back(back, middle, cot, ffn_out, gain):
    gain = gain[None]
    return row_call(
        second_back_kernel,
        middle.shape,
        [(back, None), (middle, None), (cot, None), (ffn_out, None), (gain, whole_block(gain))],
        [("rows", BF16), ("rows", F32), ("rows", BF16), ("gain", F32)],
        [],
        "second_back",
    )


def first_back(rows, grad_middle, gain, parts):
    gain = gain[None]
    specs, starts = part_specs([terms[0] for terms in parts])
    operands = [(rows, None), (grad_middle, None), (gain, whole_block(gain))]
    for terms, spec in zip(parts, specs):
        operands += [(term, spec) for term in terms]
    return row_call(
        functools.partial(first_back_kernel, starts, len(parts[0])),
        rows.shape,
        operands,
        [("rows", BF16), ("gain", F32)],
        [pltpu.VMEM((ROWS, rows.shape[1]), F32)],
        "first_back",
    )


def after(array, other):
    return lax.optimization_barrier((array, other))[0]


def turn(array, axis, shift):
    size = lax.axis_size(axis)
    return lax.ppermute(array, axis, [((i + shift) % size, i) for i in range(size)])


def partner(array, axis, bit):
    return lax.ppermute(array, axis, [(i, i ^ bit) for i in range(lax.axis_size(axis))])


def is_power(size):
    return size & (size - 1) == 0


def sum_small(array, axis):
    size = lax.axis_size(axis)
    if not is_power(size):
        return lax.psum(array, axis)
    bit = 1
    while bit < size:
        array = array + partner(array, axis, bit)
        bit *= 2
    return array


def scatter_sum_dp(array, meanwhile=None):
    size = lax.axis_size("dp")
    if not is_power(size):
        return lax.psum_scatter(array, "dp", scatter_dimension=0, tiled=True)
    index = lax.axis_index("dp")
    columns = array.shape[1]
    blocks = array.reshape(size, -1, columns)
    bit = 1
    while bit < size:
        halves = blocks.reshape(-1, 2, blocks.shape[1], columns)
        mine = (index // bit) % 2
        keep = lax.dynamic_index_in_dim(halves, mine, 1, keepdims=False)
        send = lax.dynamic_index_in_dim(halves, 1 - mine, 1, keepdims=False)
        other = partner(send, "dp", bit)
        if bit == 2 and meanwhile is not None:
            other = after(other, meanwhile)
        blocks = keep + other
        bit *= 2
    return blocks[0]


def shards(
    residual_in,
    mixer_gain,
    in_weight,
    rate_weight,
    conv_weight,
    decay_log,
    decay_bias,
    head_gain,
    out_weight,
    ffn_gain,
    gate_up,
    down_weight,
    segments,
    pad_mask,
    out_grad,
):
    rows_here, model_width = residual_in.shape
    heads_here, in_width = in_weight.shape[1:]
    hidden_here = gate_up.shape[2]
    members = lax.axis_size("tensor")
    share = lax.axis_size("dp")
    index = lax.axis_index("dp")
    pair = members == 2 and rows_here == SEQ
    value_dim = head_gain.shape[0]
    key_dim = (conv_weight.shape[2] - value_dim) // 2

    def sequences(rows):
        if pair:
            own = [rows[at : at + PART] for at in range(0, SEQ, PART)]
            return [own, [turn(part, "tensor", 1) for part in own]]
        whole = lax.all_gather(rows, "tensor", axis=0, tiled=True)
        return [
            [whole[at + by : at + by + PART] for by in range(0, SEQ, PART)]
            for at in range(0, whole.shape[0], SEQ)
        ]

    def token_parts(array):
        if pair:
            own = lax.axis_index("tensor")
            return [
                lax.dynamic_slice_in_dim(array, which * SEQ, SEQ) for which in (own, 1 - own)
            ]
        return [array[at : at + SEQ] for at in range(0, array.shape[0], SEQ)]

    def owner_parts(parts):
        if pair:
            return [[mine, other] for mine, other in zip(*parts)]
        return [
            [
                lax.psum_scatter(
                    jnp.concatenate([part for here in parts for part in here]).astype(BF16),
                    "tensor",
                    scatter_dimension=0,
                    tiled=True,
                )
            ]
        ]

    w_in = in_weight.reshape(model_width, heads_here * in_width)
    w_rate = rate_weight.transpose(2, 1, 0).reshape(2 * heads_here, model_width)
    w_out = out_weight.reshape(-1, model_width)
    conv_float = conv_weight.astype(F32)
    gain_row = head_gain[None]
    normed = norm_rows(residual_in, mixer_gain)

    rows_share = model_width // share
    gate_up_piece = lax.dynamic_slice_in_dim(gate_up, index * rows_share, rows_share)
    piece = jnp.stack(
        [
            gate_up_piece[:, 0],
            gate_up_piece[:, 1],
            lax.dynamic_slice_in_dim(down_weight, index * rows_share, rows_share, axis=1).T,
        ]
    )
    pieces = [piece] + [
        after(turn(piece, "tensor", shift), normed) for shift in range(1, members)
    ]
    pieces = jnp.concatenate(
        [part[kind] for kind in range(3) for part in pieces], axis=1
    )
    weights = lax.all_gather(pieces, "dp", axis=0, tiled=True)
    first = sequences(normed)


    tables = [
        segment_tables(seg, mask, BLOCK)
        for seg, mask in zip(token_parts(segments), token_parts(pad_mask))
    ]
    local = len(first)
    count = SEQ // PART
    states = [jnp.zeros((heads_here, key_dim, value_dim), F32)] * local
    befores = [jnp.zeros((HALO, heads_here * in_width), BF16)] * local
    forward = [[None] * count for unused in range(local)]
    out_parts = [[None] * count for unused in range(local)]
    if pair:
        order = [(0, 0)] + [(1, p) for p in range(count)] + [(0, p) for p in range(1, count)]
    else:
        order = [(s, p) for p in range(count) for s in range(local)]
    done = None
    for place, (s, p) in enumerate(order):
            low_rows = first[s][p]
            if done is not None:
                low_rows = after(low_rows, done)
            if pair and place == len(order) - 1:
                low_rows = after(low_rows, arrived)
            projected = dot_nn(low_rows, w_in).astype(BF16)
            rate_rows = dot_nt(w_rate, low_rows).reshape(2, heads_here, PART)
            cols, rows, log_decay = token_tables(
                rate_rows, tables[s][:, p * PART : (p + 1) * PART], decay_log, decay_bias, BLOCK
            )
            gated, *kept, states[s] = mixer_forward(
                projected, befores[s], cols, rows, conv_float, gain_row, states[s], BLOCK
            )
            forward[s][p] = (
                projected, befores[s], rate_rows, cols, rows, log_decay, gated, kept
            )
            befores[s] = projected[-HALO:]
            out_parts[s][p] = dot_nn(gated, w_out)
            done = out_parts[s][p]
            if pair and s == 1:
                out_parts[s][p] = turn(out_parts[s][p].astype(BF16), "tensor", 1)
                if p < count - 1:
                    arrived = out_parts[s][p]
    middle, second, second_turned = middle_rows(residual_in, ffn_gain, owner_parts(out_parts))
    ffn_out, grad_second, grads_ffn = feed_forward(
        second, second_turned, out_grad, weights, share
    )
    ffn_shares = lax.psum_scatter(
        grads_ffn.reshape(-1, grads_ffn.shape[-1]), "dp", scatter_dimension=0, tiled=True
    )
    layer_out, grad_middle, grad_mix, grad_ffn_gain = second_back(
        grad_second, middle, out_grad, ffn_out, ffn_gain
    )
    cots = sequences(grad_mix)
    every = [(s, p) for s in range(local) for p in range(count)]
    gated_all = jnp.concatenate([forward[s][p][6] for s, p in every])
    cots_all = jnp.concatenate([cots[s][p] for s, p in every])
    grad_out = dot_tn(gated_all, cots_all).astype(BF16)
    grad_states = [jnp.zeros((heads_here, key_dim, value_dim), F32)] * local
    afters = [jnp.zeros((heads_here, HALO, conv_weight.shape[2]), F32)] * local
    first_parts = [[None] * count for unused in range(local)]
    proj_lows = [[None] * count for unused in range(local)]
    grad_rate, sums = 0.0, 0.0
    done = None
    for place, (s, p) in enumerate(reversed(order)):
            projected, before, rate_rows, cols, rows, log_decay, gated, kept = forward[s][p]
            grad_gated = dot_nt(cots[s][p], w_out).astype(BF16)
            if done is not None:
                grad_gated = after(grad_gated, done)
            if place == local * count // 2:
                grad_gated = after(grad_gated, grad_out)
            proj_low, tokens, colsum, grad_conv, grad_head_gain, grad_states[s], afters[s] = (
                mixer_backward(
                    grad_gated, projected, before, cols, rows, conv_float, gain_row, kept,
                    grad_states[s], afters[s], BLOCK,
                )
            )
            grad_rates, grad_log, grad_bias = rate_gradients(
                tokens, colsum, rate_rows, tables[s][0, p * PART : (p + 1) * PART],
                decay_log, decay_bias, log_decay, BLOCK,
            )
            rates_low = grad_rates.astype(BF16).reshape(2 * heads_here, PART)
            grad_rate = grad_rate + dot_nn(rates_low, first[s][p])
            first_parts[s][p] = dot_nt(proj_low, w_in) + dot_tn(rates_low, w_rate)
            proj_lows[s][p] = after(proj_low, first_parts[s][p])
            done = first_parts[s][p]
            if pair and s == 1:
                first_parts[s][p] = turn(first_parts[s][p].astype(BF16), "tensor", 1)
            sums = sums + jnp.concatenate(
                [grad_conv.reshape(-1), grad_head_gain[0], grad_log, grad_bias]
            )
    input_grad, grad_mixer_gain = first_back(
        residual_in, grad_middle, mixer_gain, owner_parts(first_parts)
    )
    share_out = scatter_sum_dp(grad_out)
    proj_lows[0][0] = after(proj_lows[0][0], share_out)
    grad_in = in_grad(
        [first[s][p] for s, p in every], [proj_lows[s][p] for s, p in every], in_width
    )
    ffn_shares = after(ffn_shares, done)
    share_ffn = ffn_shares[:, :hidden_here]
    for shift in range(1, members):
        share_ffn = share_ffn + turn(
            ffn_shares[:, shift * hidden_here : (shift + 1) * hidden_here], "tensor", -shift
        )
    share_ffn = share_ffn.reshape(3, rows_share, hidden_here)
    share_early = jnp.concatenate([*share_ffn, share_out.reshape(rows_share, -1)], axis=1)
    early = lax.all_gather(share_early, "dp", axis=0, tiled=True)
    if pair:
        grad_in = after(grad_in, first_parts[1])
    grad_in = after(grad_in, share_early)

    small = jnp.concatenate([sums, grad_rate.reshape(-1), grad_mixer_gain[0], grad_ffn_gain[0]])
    length = small.shape[0]
    small = jnp.pad(small, (0, -length % 1024)).reshape(-1, 1024)
    small = sum_small(small, "dp").reshape(-1)
    share_in = scatter_sum_dp(grad_in, small)
    conv_size = conv_weight.size
    rate_size = rate_weight.size
    grad_conv = small[:conv_size].reshape(conv_weight.shape)
    at = conv_size + value_dim
    grad_log = small[at : at + heads_here]
    grad_bias = small[at + heads_here : at + 2 * heads_here]
    at += 2 * heads_here
    grad_rate = small[at : at + rate_size].reshape(2, heads_here, model_width).transpose(2, 1, 0)
    at += rate_size
    gains = jnp.concatenate([small[conv_size : conv_size + value_dim], small[at:length]])
    gains = sum_small(gains, "tensor")
    grad_head_gain = gains[:value_dim]
    grad_mixer_gain = gains[value_dim : value_dim + model_width]
    grad_ffn_gain = gains[value_dim + model_width :]

    share_in = share_in.reshape(rows_share, heads_here, in_width)
    grad_in = lax.all_gather(share_in, "dp", axis=0, tiled=True)
    width = 2 * hidden_here
    grad_gate_up = early[:, :width].reshape(gate_up.shape).astype(F32)
    grad_down = early[:, width : width + hidden_here].astype(F32).T
    grad_out = early[:, width + hidden_here :].astype(F32).reshape(out_weight.shape)
    grad_in = after(grad_in, (grad_gate_up, grad_down, grad_out)).astype(F32)
    return (
        layer_out,
        input_grad,
        grad_mixer_gain,
        grad_in,
        grad_rate,
        grad_conv,
        grad_log,
        grad_bias,
        grad_head_gain,
        grad_out,
        grad_ffn_gain,
        grad_gate_up,
        grad_down,
    )


def solution(mesh):
    return jax.shard_map(
        shards,
        mesh=mesh,
        in_specs=(
            P(("dp", "tensor"), None),
            P(),
            P(None, "tensor", None),
            P(None, "tensor", None),
            P("tensor", None, None),
            P("tensor"),
            P("tensor"),
            P(),
            P("tensor", None, None),
            P(),
            P(None, None, "tensor"),
            P("tensor", None),
            P("dp"),
            P("dp"),
            P(("dp", "tensor"), None),
        ),
        out_specs=(
            P(("dp", "tensor"), None),
            P(("dp", "tensor"), None),
            P(),
            P(None, "tensor", None),
            P(None, "tensor", None),
            P("tensor", None, None),
            P("tensor"),
            P("tensor"),
            P(),
            P("tensor", None, None),
            P(),
            P(None, None, "tensor"),
            P("tensor", None),
        ),
        check_vma=False,
    )
```

```python
import functools

import jax
import jax.numpy as jnp
from jax import lax
from jax.experimental import pallas as pl
from jax.experimental.pallas import tpu as pltpu
from jax.sharding import PartitionSpec as P

SEQ = 1024
BLOCK = 256
PART = 512
LANES = 128
HALO = 16
F32 = jnp.float32
BF16 = jnp.bfloat16
VMEM_BYTES = 56 * 1024 * 1024
MIXER_VMEM_BYTES = 56 * 1024 * 1024


def dot_nn(left, right):
    return lax.dot_general(left, right, (((1,), (0,)), ((), ())), preferred_element_type=F32)


def dot_nt(left, right):
    return lax.dot_general(left, right, (((1,), (1,)), ((), ())), preferred_element_type=F32)


def dot_tn(left, right):
    return lax.dot_general(left, right, (((0,), (0,)), ((), ())), preferred_element_type=F32)


def sigmoid(values):
    return 0.5 * jnp.tanh(0.5 * values) + 0.5


def row_sum(values):
    return jnp.sum(values, axis=1, keepdims=True)


MASK, BACK, AHEAD, SEGMENT, CARRIED, TO_LAST = 0, 1, 4, 7, 8, 9
WRITE, CUM, START, LAST = 8, 16, 24, 32
SLOTS = 8


def fill_level_masks(mask_ref):
    levels, width, unused_width = mask_ref.shape
    later = lax.broadcasted_iota(jnp.int32, (width, width), 0)
    earlier = lax.broadcasted_iota(jnp.int32, (width, width), 1)
    apart = later ^ earlier
    for level in range(levels):
        chosen = (later > earlier) & ((apart >> level) == 1)
        mask_ref[level] = jnp.where(chosen, 1.0, 0.0).astype(BF16)


def unit_lower_inverses(systems, mask_ref):
    width = systems[0].shape[0]
    identity = jnp.where(
        lax.broadcasted_iota(jnp.int32, (width, width), 0)
        == lax.broadcasted_iota(jnp.int32, (width, width), 1),
        1.0,
        0.0,
    ).astype(BF16)
    inverses = [identity - system * mask_ref[0] for system in systems]
    level = 1
    while (2 << level) <= width:
        size = 1 << level
        if size < 16:
            halves = [dot_nn(inv, system).astype(BF16) for inv, system in zip(inverses, systems)]
            joined = [dot_nn(half, inv).astype(BF16) for half, inv in zip(halves, inverses)]
            inverses = [inv - both * mask_ref[level] for inv, both in zip(inverses, joined)]
        elif (2 << level) < width:
            starts = range(size, width, 2 * size)
            odd = [
                jnp.concatenate([inv[at : at + size] for at in starts], axis=0) for inv in inverses
            ]
            halves = [dot_nn(rows, system).astype(BF16) for rows, system in zip(odd, systems)]
            joined = [dot_nn(half, inv).astype(BF16) for half, inv in zip(halves, inverses)]
            chosen = jnp.concatenate([mask_ref[level, at : at + size, :] for at in starts], axis=0)
            odd = [rows - both * chosen for rows, both in zip(odd, joined)]
            inverses = [
                jnp.concatenate(
                    [
                        part
                        for place, at in enumerate(starts)
                        for part in (
                            inv[at - size : at],
                            rows[place * size : (place + 1) * size],
                        )
                    ],
                    axis=0,
                )
                for inv, rows in zip(inverses, odd)
            ]
        else:
            halves = [
                dot_nn(inv[size:, size:], system[size:, :size]).astype(BF16)
                for inv, system in zip(inverses, systems)
            ]
            joined = [
                dot_nn(half, inv[:size, :size]).astype(BF16) for half, inv in zip(halves, inverses)
            ]
            inverses = [
                jnp.concatenate(
                    [inv[:size], jnp.concatenate([-both, inv[size:, size:]], axis=1)], axis=0
                )
                for inv, both in zip(inverses, joined)
            ]
        level += 1
    return inverses


def conv_rows(padded_ref, head, cols, conv_ref):
    width = cols.shape[0]
    taps = conv_ref.shape[1]
    shifted = [padded_ref[head, HALO : HALO + width, :]]
    for offset in range(1, taps):
        usable = cols[:, BACK + offset - 1 : BACK + offset]
        shifted.append(padded_ref[head, HALO - offset : HALO - offset + width, :] * usable)
    summed = shifted[0] * conv_ref[head, 0:1, :]
    for offset in range(1, taps):
        summed = summed + shifted[offset] * conv_ref[head, offset : offset + 1, :]
    return summed, shifted


def gap_offsets(cols, rows):
    width = cols.shape[0]
    later = lax.broadcasted_iota(jnp.int32, (width, width), 0)
    earlier = lax.broadcasted_iota(jnp.int32, (width, width), 1)
    inside = (cols[:, SEGMENT : SEGMENT + 1] == rows[0:1, :]) & (later >= earlier)
    return jnp.where(inside, 0.0, -1e30)


def head_column(cols, head, which):
    return cols[:, which + head : which + head + 1]


def softplus(values):
    return jnp.maximum(values, 0.0) + jnp.log1p(jnp.exp(-jnp.abs(values)))


def exact_dot(left, right):
    return lax.dot_general(
        left, right, (((1,), (0,)), ((), ())), precision=lax.Precision.HIGHEST,
        preferred_element_type=F32,
    )


def triangle(width, upper):
    one = lax.broadcasted_iota(jnp.int32, (width, width), 0)
    other = lax.broadcasted_iota(jnp.int32, (width, width), 1)
    return jnp.where(one <= other if upper else one >= other, 1.0, 0.0)


def fwd_kernel(
    low_ref, before_ref, table_ref, w_in_ref, w_rate_ref, w_out_ref, decay_ref,
    conv_ref, gain_ref, initial_ref,
    part_ref, proj_ref, rates_ref, cols_ref, gated_ref, out_ref, written_ref, inverse_ref,
    start_ref, state_ref,
    padded_ref, mask_ref,
):
    heads, taps, mix_width = conv_ref.shape
    value_dim = gain_ref.shape[1]
    key_dim = (mix_width - value_dim) // 2
    in_width = mix_width + value_dim
    width = low_ref.shape[0]
    block = pl.program_id(0)
    every = range(heads)

    @pl.when(block == 0)
    def _():
        fill_level_masks(mask_ref)
        state_ref[...] = initial_ref[...]
        for h in range(heads):
            at = h * in_width
            padded_ref[h, 0:HALO, :] = before_ref[:, at : at + mix_width].astype(F32)

    @pl.when(block > 0)
    def _():
        for h in range(heads):
            padded_ref[h, 0:HALO, :] = padded_ref[h, width : width + HALO, :]

    low = low_ref[...]
    gates = []
    for h in every:
        at = h * in_width
        projected = dot_nn(low, w_in_ref[:, at : at + in_width])
        proj_ref[:, at : at + in_width] = projected.astype(BF16)
        padded_ref[h, HALO : HALO + width, :] = projected[:, :mix_width]
        gates.append(projected[:, mix_width:])

    table = table_ref[...]
    rates = dot_nt(w_rate_ref[...], low)
    rates_ref[...] = rates
    log_decay = decay_ref[:, 0:1] * softplus(rates[:SLOTS] + decay_ref[:, 1:2])
    cum = exact_dot(log_decay, triangle(width, True))
    write = sigmoid(rates[SLOTS:]) * table[MASK : MASK + 1]
    start = jnp.exp(cum) * table[CARRIED : CARRIED + 1]
    last = jnp.exp(cum[:, width - 1 : width] - cum) * table[TO_LAST : TO_LAST + 1]
    cols = jnp.concatenate([table[:SLOTS], write, cum, start, last], axis=0).T
    cols_ref[...] = cols
    offsets = gap_offsets(cols, table[SEGMENT : SEGMENT + 1])

    queries, keys, values = [], [], []
    for h in every:
        summed, unused_rows = conv_rows(padded_ref, h, cols, conv_ref)
        mixed = summed * sigmoid(summed)
        query = mixed[:, :key_dim]
        key = mixed[:, key_dim : 2 * key_dim]
        query = query * (lax.rsqrt(row_sum(query * query) + 1e-06) * key_dim ** (-0.5))
        key = key * lax.rsqrt(row_sum(key * key) + 1e-06)
        queries.append(query.astype(BF16))
        keys.append(key)
        values.append(mixed[:, 2 * key_dim :])
    keys_low = [key.astype(BF16) for key in keys]
    stacked = [jnp.concatenate([k, q], axis=0) for k, q in zip(keys_low, queries)]
    products = [dot_nt(both, key) for both, key in zip(stacked, keys_low)]
    weights = [jnp.exp(head_column(cols, h, CUM) - cum[h : h + 1, :] + offsets) for h in every]
    systems = [
        (products[h][:width] * weights[h] * head_column(cols, h, WRITE)).astype(BF16)
        for h in every
    ]
    reads = [(products[h][width:] * weights[h]).astype(BF16) for h in every]
    inverses = unit_lower_inverses(systems, mask_ref)
    states = [state_ref[h] for h in every]
    states_low = [state.astype(BF16) for state in states]
    from_state = [dot_nn(both, state) for both, state in zip(stacked, states_low)]
    right = [
        (
            head_column(cols, h, WRITE)
            * (values[h] - head_column(cols, h, START) * from_state[h][:width])
        ).astype(BF16)
        for h in every
    ]
    written = [dot_nn(inv, side).astype(BF16) for inv, side in zip(inverses, right)]
    inner = [dot_nn(read, value) for read, value in zip(reads, written)]
    added = [
        dot_tn((keys[h] * head_column(cols, h, LAST)).astype(BF16), written[h]) for h in every
    ]
    keep = cols[:, MASK : MASK + 1]
    for h in every:
        start_ref[0, h] = states_low[h]
        inverse_ref[0, h] = inverses[h]
        written_ref[:, h * value_dim : (h + 1) * value_dim] = written[h]
        final = head_column(cols, h, START)[width - 1 : width, :]
        state_ref[h] = final * states[h] + added[h]
        out = (inner[h] + head_column(cols, h, START) * from_state[h][width:]) * keep
        out_ref[:, h * value_dim : (h + 1) * value_dim] = out.astype(BF16)
        scale = lax.rsqrt(row_sum(out * out) * (1.0 / value_dim) + 1e-05)
        gate = gates[h]
        gated = out * scale * gain_ref[...] * (gate * sigmoid(gate))
        gated_ref[:, h * value_dim : (h + 1) * value_dim] = gated.astype(BF16)
    part_ref[...] = dot_nn(gated_ref[...], w_out_ref[...]).astype(part_ref.dtype)


def bwd_kernel(
    cot_ref, low_ref, proj_ref, halo_ref, before_ref, table_ref, rates_ref, cols_ref,
    w_in_ref, w_rate_ref, w_out_ref, decay_ref, conv_ref, gain_ref,
    out_ref, written_ref, inverse_ref, start_ref, initial_ref, after_ref,
    part_ref, grad_ref, conv_grad_ref, gain_grad_ref, rate_grad_ref, decay_grad_ref,
    state_ref, stash_ref,
    padded_ref, ahead_ref,
):
    heads, taps, mix_width = conv_ref.shape
    value_dim = gain_ref.shape[1]
    key_dim = (mix_width - value_dim) // 2
    in_width = mix_width + value_dim
    width = proj_ref.shape[0]
    step = pl.program_id(0)
    first = step == pl.num_programs(0) - 1
    every = range(heads)

    @pl.when(step == 0)
    def _():
        conv_grad_ref[...] = jnp.zeros_like(conv_grad_ref)
        gain_grad_ref[...] = jnp.zeros_like(gain_grad_ref)
        rate_grad_ref[...] = jnp.zeros_like(rate_grad_ref)
        decay_grad_ref[...] = jnp.zeros_like(decay_grad_ref)
        state_ref[...] = initial_ref[...]
        ahead_ref[:, width : width + HALO, :] = after_ref[...]

    @pl.when(first)
    def _():
        for h in range(heads):
            at = h * in_width
            padded_ref[h, 0:HALO, :] = before_ref[:, at : at + mix_width].astype(F32)

    @pl.when(jnp.logical_not(first))
    def _():
        for h in range(heads):
            at = h * in_width
            padded_ref[h, 0:HALO, :] = halo_ref[:, at : at + mix_width].astype(F32)

    cols = cols_ref[...]
    table = table_ref[...]
    offsets = gap_offsets(cols, table[SEGMENT : SEGMENT + 1])
    rates = rates_ref[...]
    log_decay = decay_ref[:, 0:1] * softplus(rates[:SLOTS] + decay_ref[:, 1:2])
    cum = exact_dot(log_decay, triangle(width, True))
    keep = cols[:, MASK : MASK + 1]
    strict = (
        lax.broadcasted_iota(jnp.int32, (width, width), 0)
        > lax.broadcasted_iota(jnp.int32, (width, width), 1)
    )

    cots, gain_grad = [], jnp.zeros((1, value_dim), F32)
    for h in every:
        at = h * in_width + mix_width
        cot = dot_nt(cot_ref[...], w_out_ref[h * value_dim : (h + 1) * value_dim, :])
        out = out_ref[:, h * value_dim : (h + 1) * value_dim].astype(F32)
        gate = proj_ref[:, at : at + value_dim].astype(F32)
        scale = lax.rsqrt(row_sum(out * out) * (1.0 / value_dim) + 1e-05)
        gate_sig = sigmoid(gate)
        normed = out * scale
        through = cot * gate * gate_sig
        gain_grad = gain_grad + jnp.sum(through * normed, axis=0, keepdims=True)
        grad_normed = through * gain_ref[...]
        mean = row_sum(grad_normed * normed) * (1.0 / value_dim)
        cots.append((scale * (grad_normed - normed * mean) * keep))
        grad_gate = cot * normed * gain_ref[...] * gate_sig * (1.0 + gate * (1.0 - gate_sig))
        grad_ref[:, at : at + value_dim] = grad_gate.astype(BF16)
    gain_grad_ref[...] += gain_grad

    queries, keys = [], []
    for h in every:
        at = h * in_width
        padded_ref[h, HALO : HALO + width, :] = proj_ref[:, at : at + mix_width].astype(F32)
        summed, unused_rows = conv_rows(padded_ref, h, cols, conv_ref)
        qk = summed[:, : 2 * key_dim]
        mixed = qk * sigmoid(qk)
        query = mixed[:, :key_dim]
        key = mixed[:, key_dim:]
        query = query * (lax.rsqrt(row_sum(query * query) + 1e-06) * key_dim ** (-0.5))
        key = key * lax.rsqrt(row_sum(key * key) + 1e-06)
        queries.append(query)
        keys.append(key)
        ahead_ref[h, 0:width, :] = summed
    keys_low = [key.astype(BF16) for key in keys]
    queries_low = [query.astype(BF16) for query in queries]
    products = [
        dot_nt(jnp.concatenate([k, q], axis=0), k) for k, q in zip(keys_low, queries_low)
    ]
    weights = [jnp.exp(head_column(cols, h, CUM) - cum[h : h + 1, :] + offsets) for h in every]
    cots_low = [cot.astype(BF16) for cot in cots]
    grad_states = [state_ref[h] for h in every]
    grad_states_low = [state.astype(BF16) for state in grad_states]
    written = [written_ref[:, h * value_dim : (h + 1) * value_dim] for h in every]
    reads = [(products[h][width:] * weights[h]).astype(BF16) for h in every]
    last_keys = [keys[h] * head_column(cols, h, LAST) for h in every]
    grad_written = [
        (
            dot_tn(reads[h], cots_low[h]) + dot_nn(last_keys[h].astype(BF16), grad_states_low[h])
        ).astype(BF16)
        for h in every
    ]
    grad_right = [dot_tn(inverse_ref[0, h], grad_written[h]) for h in every]
    grad_values = [grad_right[h] * head_column(cols, h, WRITE) for h in every]
    against = [
        dot_nt(jnp.concatenate([cots_low[h], grad_right[h].astype(BF16)], axis=0), written[h])
        for h in every
    ]
    grad_reads = [against[h][:width] * weights[h] for h in every]
    grad_pairs = [
        jnp.where(strict, against[h][width:] * weights[h], 0.0) * -head_column(cols, h, WRITE)
        for h in every
    ]
    gaps = [
        grad_reads[h] * products[h][width:] + grad_pairs[h] * products[h][:width] for h in every
    ]
    starts = [
        jnp.concatenate(
            [
                (cots[h] * head_column(cols, h, START)).astype(BF16),
                (grad_values[h] * -head_column(cols, h, START)).astype(BF16),
            ],
            axis=0,
        )
        for h in every
    ]
    both_grads = [
        jnp.concatenate([grad_reads[h].astype(BF16), grad_pairs[h].astype(BF16)], axis=0)
        for h in every
    ]
    by_key = [dot_nn(both_grads[h], keys_low[h]) for h in every]
    by_state = [dot_nt(starts[h], start_ref[0, h]) for h in every]
    both_rows = [jnp.concatenate([queries_low[h], keys_low[h]], axis=0) for h in every]
    turned = [dot_tn(both_grads[h], both_rows[h]) for h in every]
    by_last = [dot_nt(written[h], grad_states_low[h]) for h in every]
    states_part = [dot_tn(both_rows[h], starts[h]) for h in every]

    lane = lax.broadcasted_iota(jnp.int32, (width, 2 * SLOTS), 1)
    place = lax.broadcasted_iota(jnp.int32, (width, 1), 0)
    packed = jnp.zeros((width, 2 * SLOTS), F32)
    slot = lax.broadcasted_iota(jnp.int32, (SLOTS, width), 0)
    column_sums = jnp.zeros((SLOTS, width), F32)
    for h in every:
        from_state = by_state[h]
        grad_query = by_key[h][:width] + from_state[:width]
        grad_key = (
            by_key[h][width:]
            + from_state[width:]
            + turned[h]
            + by_last[h] * head_column(cols, h, LAST)
        )
        log_last = row_sum(by_last[h] * last_keys[h])
        log_start = row_sum(queries[h] * from_state[:width] + keys[h] * from_state[width:])
        final = head_column(cols, h, START)[width - 1 : width, :]
        start_f32 = start_ref[0, h].astype(F32)
        total = jnp.sum(log_last, axis=0, keepdims=True) + final * jnp.sum(
            row_sum(start_f32 * grad_states[h]), axis=0, keepdims=True
        )
        grad_cum = row_sum(gaps[h]) + log_start - log_last + jnp.where(
            place == width - 1, total, 0.0
        )
        grad_logit = row_sum(grad_right[h] * written[h].astype(F32))
        packed = packed + jnp.where(lane == h, grad_cum, 0.0)
        packed = packed + jnp.where(lane == SLOTS + h, grad_logit, 0.0)
        column_sums = column_sums + jnp.where(
            slot == h, jnp.sum(gaps[h], axis=0, keepdims=True), 0.0
        )
        state_ref[h] = final * grad_states[h] + states_part[h]

        summed = ahead_ref[h, 0:width, :]
        sig = sigmoid(summed)
        slope = sig * (1.0 + summed * (1.0 - sig))
        mixed = summed[:, : 2 * key_dim] * sig[:, : 2 * key_dim]
        query = mixed[:, :key_dim]
        key = mixed[:, key_dim:]
        query_scale = lax.rsqrt(row_sum(query * query) + 1e-06)
        key_scale = lax.rsqrt(row_sum(key * key) + 1e-06)
        grad_query = grad_query * key_dim ** (-0.5)
        query_unit = query * query_scale
        key_unit = key * key_scale
        grad_query = query_scale * (grad_query - query_unit * row_sum(grad_query * query_unit))
        grad_key = key_scale * (grad_key - key_unit * row_sum(grad_key * key_unit))
        ahead_ref[h, 0:width, 0:key_dim] = grad_query * slope[:, :key_dim]
        ahead_ref[h, 0:width, key_dim : 2 * key_dim] = (
            grad_key * slope[:, key_dim : 2 * key_dim]
        )
        ahead_ref[h, 0:width, 2 * key_dim :] = grad_values[h] * slope[:, 2 * key_dim :]
        grad_summed = ahead_ref[h, 0:width, :]
        at = h * in_width
        grad_pre = grad_summed * conv_ref[h, 0:1, :]
        conv_grad_ref[h, 0:1, :] += jnp.sum(
            grad_summed * padded_ref[h, HALO : HALO + width, :], axis=0, keepdims=True
        )
        for offset in range(1, taps):
            usable = cols[:, AHEAD + offset - 1 : AHEAD + offset]
            later = ahead_ref[h, offset : offset + width, :] * usable
            grad_pre = grad_pre + later * conv_ref[h, offset : offset + 1, :]
            back = cols[:, BACK + offset - 1 : BACK + offset]
            earlier = padded_ref[h, HALO - offset : HALO - offset + width, :] * back
            conv_grad_ref[h, offset : offset + 1, :] += jnp.sum(
                grad_summed * earlier, axis=0, keepdims=True
            )
        grad_ref[:, at : at + mix_width] = grad_pre.astype(BF16)
        ahead_ref[h, width : width + HALO, :] = ahead_ref[h, 0:HALO, :]
        stash_ref[h] = ahead_ref[h, 0:HALO, :]

    turned_rows = packed.T
    grad_log_decay = exact_dot(turned_rows[:SLOTS] - column_sums, triangle(width, False))
    shifted = rates[:SLOTS] + decay_ref[:, 1:2]
    grad_decay = grad_log_decay * decay_ref[:, 0:1] * sigmoid(shifted)
    grad_write = (
        turned_rows[SLOTS:] * (1.0 - sigmoid(rates[SLOTS:])) * table[MASK : MASK + 1]
    )
    decay_grad_ref[0:SLOTS, :] += grad_log_decay * log_decay
    decay_grad_ref[SLOTS : 2 * SLOTS, :] += grad_decay
    grad_rates = jnp.concatenate([grad_decay, grad_write], axis=0).astype(BF16)
    rate_grad_ref[...] += dot_nn(grad_rates, low_ref[...])
    part_ref[...] = (
        dot_nt(grad_ref[...], w_in_ref[...]) + dot_tn(grad_rates, w_rate_ref[...])
    ).astype(part_ref.dtype)


def segment_tables(segments, pad_mask, width):
    length = segments.shape[0]
    place = jnp.arange(length, dtype=jnp.int32)

    def moved(array, by):
        if by > 0:
            return jnp.concatenate([jnp.full((by,), -1, array.dtype), array[:-by]])
        return jnp.concatenate([array[-by:], jnp.full((-by,), -1, array.dtype)])

    back = [
        ((moved(segments, by) == segments) & (place >= by)).astype(F32) for by in (1, 2, 3)
    ]
    ahead = [
        ((moved(segments, -by) == segments) & (place + by < length)).astype(F32)
        for by in (1, 2, 3)
    ]
    seg_blocks = segments.reshape(-1, width)
    ends = seg_blocks[:, -1]
    carried = (seg_blocks == moved(ends, 1)[:, None]).astype(F32).reshape(-1)
    to_last = (seg_blocks == ends[:, None]).astype(F32).reshape(-1)
    rows = [pad_mask.astype(F32), *back, *ahead, segments.astype(F32), carried, to_last]
    return jnp.concatenate([jnp.stack(rows), jnp.zeros((-len(rows) % SLOTS, length), F32)])


def whole_block(array):
    return pl.BlockSpec(array.shape, lambda c: (0,) * array.ndim)


def kept_block(array):
    return pl.BlockSpec(
        array.shape, lambda c: (0,) * array.ndim, pipeline_mode=pl.Buffered(1)
    )


def last_rows(array):
    return pl.BlockSpec((HALO, array.shape[1]), lambda c: (array.shape[0] // HALO - 1, 0))


def mixer_forward(low, before, table, weights, decay, conv, gain, initial, width, part_dtype):
    heads, taps, mix_width = conv.shape
    value_dim = gain.shape[1]
    key_dim = (mix_width - value_dim) // 2
    in_width = heads * (mix_width + value_dim)
    length, model_width = low.shape
    steps = length // width
    levels = width.bit_length() - 1

    def rows_of(columns):
        return pl.BlockSpec((width, columns), lambda c: (c, 0))

    def lanes_of(rows):
        return pl.BlockSpec((rows, width), lambda c: (0, c))

    def shape(dims, dtype):
        return jax.ShapeDtypeStruct(dims, dtype)

    value_width = heads * value_dim
    return pl.pallas_call(
        fwd_kernel,
        grid=(steps,),
        in_specs=[rows_of(model_width), last_rows(before), lanes_of(table.shape[0])]
        + [kept_block(array) for array in weights]
        + [whole_block(array) for array in (decay, conv, gain, initial)],
        out_specs=[
            rows_of(model_width),
            rows_of(in_width),
            lanes_of(2 * SLOTS),
            rows_of(5 * SLOTS),
            rows_of(value_width),
            rows_of(value_width),
            rows_of(value_width),
            pl.BlockSpec((1, heads, width, width), lambda c: (c, 0, 0, 0)),
            pl.BlockSpec((1, heads, key_dim, value_dim), lambda c: (c, 0, 0, 0)),
            whole_block(initial),
        ],
        out_shape=[
            shape((length, model_width), part_dtype),
            shape((length, in_width), BF16),
            shape((2 * SLOTS, length), F32),
            shape((length, 5 * SLOTS), F32),
            shape((length, value_width), BF16),
            shape((length, value_width), BF16),
            shape((length, value_width), BF16),
            shape((steps, heads, width, width), BF16),
            shape((steps, heads, key_dim, value_dim), BF16),
            shape(initial.shape, F32),
        ],
        scratch_shapes=[
            pltpu.VMEM((heads, HALO + width, mix_width), F32),
            pltpu.VMEM((levels, width, width), BF16),
        ],
        compiler_params=pltpu.CompilerParams(vmem_limit_bytes=MIXER_VMEM_BYTES),
        cost_estimate=pl.CostEstimate(
            flops=length * model_width * 1024, bytes_accessed=length * 1024, transcendentals=0
        ),
        name="mixer_forward",
    )(low, before, table, *weights, decay, conv, gain, initial)


def mixer_backward(
    cot, low, table, weights, decay, conv, gain, kept, initial, after, width, part_dtype
):
    before, proj, rates, cols, out, written, inverse, start = kept
    heads, taps, mix_width = conv.shape
    value_dim = gain.shape[1]
    key_dim = (mix_width - value_dim) // 2
    length, model_width = low.shape
    steps = length // width

    def rows_of(columns):
        return pl.BlockSpec((width, columns), lambda c: (steps - 1 - c, 0))

    def lanes_of(rows):
        return pl.BlockSpec((rows, width), lambda c: (0, steps - 1 - c))

    def halo(c):
        return (jnp.maximum((steps - 1 - c) * (width // HALO) - 1, 0), 0)

    def shape(dims, dtype=F32):
        return jax.ShapeDtypeStruct(dims, dtype)

    wide = rows_of(heads * value_dim)
    rate_shape, decay_shape = (2 * SLOTS, model_width), (2 * SLOTS, width)
    fixed = [conv.shape, gain.shape, rate_shape, decay_shape, initial.shape, after.shape]
    return pl.pallas_call(
        bwd_kernel,
        grid=(steps,),
        in_specs=[
            rows_of(model_width),
            rows_of(model_width),
            rows_of(proj.shape[1]),
            pl.BlockSpec((HALO, proj.shape[1]), halo),
            last_rows(before),
            lanes_of(table.shape[0]),
            lanes_of(2 * SLOTS),
            rows_of(5 * SLOTS),
        ]
        + [kept_block(array) for array in weights]
        + [whole_block(array) for array in (decay, conv, gain)]
        + [
            wide,
            wide,
            pl.BlockSpec((1, heads, width, width), lambda c: (steps - 1 - c, 0, 0, 0)),
            pl.BlockSpec((1, heads, key_dim, value_dim), lambda c: (steps - 1 - c, 0, 0, 0)),
            whole_block(initial),
            whole_block(after),
        ],
        out_specs=[rows_of(model_width), rows_of(proj.shape[1])]
        + [pl.BlockSpec(dims, lambda c, dims=dims: (0,) * len(dims)) for dims in fixed],
        out_shape=[shape((length, model_width), part_dtype), shape(proj.shape, BF16)]
        + [shape(dims) for dims in fixed],
        scratch_shapes=[
            pltpu.VMEM((heads, HALO + width, mix_width), F32),
            pltpu.VMEM((heads, width + HALO, mix_width), F32),
        ],
        compiler_params=pltpu.CompilerParams(vmem_limit_bytes=MIXER_VMEM_BYTES),
        cost_estimate=pl.CostEstimate(
            flops=length * model_width * 1024, bytes_accessed=length * 1024, transcendentals=0
        ),
        name="mixer_backward",
    )(
        cot, low, proj, proj, before, table, rates, cols, *weights, decay, conv, gain,
        out, written, inverse, start, initial, after,
    )


def ffn_kernel(
    second_ref, second_turned_ref, cot_ref, cot_turned_ref, gate_ref, up_ref, down_ref,
    sum_ref, back_ref, grads_ref,
):
    shares, unused_kinds, rows, tile = grads_ref.shape

    @pl.when(pl.program_id(0) == 0)
    def _():
        sum_ref[...] = jnp.zeros_like(sum_ref)
        back_ref[...] = jnp.zeros_like(back_ref)

    gate = dot_nn(second_ref[...], gate_ref[...])
    up = dot_nn(second_ref[...], up_ref[...])
    grad_hidden = dot_nn(cot_ref[...], down_ref[...])
    sig = sigmoid(gate)
    active = gate * sig
    hidden = (active * up).astype(BF16)
    grad_up = (grad_hidden * active).astype(BF16)
    grad_gate = (grad_hidden * up * sig * (1.0 + gate * (1.0 - sig))).astype(BF16)
    sum_ref[...] += dot_nt(hidden, down_ref[...])
    back_ref[...] += dot_nt(grad_gate, gate_ref[...]) + dot_nt(grad_up, up_ref[...])
    for kind, (turned_ref, right) in enumerate(
        ((second_turned_ref, grad_gate), (second_turned_ref, grad_up), (cot_turned_ref, hidden))
    ):
        grads_ref[:, kind] = (
            dot_nn(turned_ref[...], right).astype(BF16).reshape(shares, rows, tile)
        )


def feed_forward(second, second_turned, cot, weights, shares):
    length, model_width = second.shape
    hidden = weights.shape[1] // 3
    tile = 256
    tiles = hidden // tile
    square = jax.ShapeDtypeStruct((length, model_width), F32)
    rows = model_width // shares

    def third(kind):
        return pl.BlockSpec((model_width, tile), lambda j: (0, kind * tiles + j))

    turned = (second_turned, cot.T)
    return pl.pallas_call(
        ffn_kernel,
        grid=(tiles,),
        in_specs=[
            whole_block(second),
            whole_block(turned[0]),
            whole_block(cot),
            whole_block(turned[1]),
            third(0),
            third(1),
            third(2),
        ],
        out_specs=[
            whole_block(square),
            whole_block(square),
            pl.BlockSpec((shares, 3, rows, tile), lambda j: (0, 0, 0, j)),
        ],
        out_shape=[square, square, jax.ShapeDtypeStruct((shares, 3, rows, hidden), BF16)],
        compiler_params=pltpu.CompilerParams(vmem_limit_bytes=VMEM_BYTES),
        cost_estimate=pl.CostEstimate(
            flops=6 * length * model_width * hidden,
            bytes_accessed=12 * model_width * hidden,
            transcendentals=0,
        ),
        name="feed_forward",
    )(second, turned[0], cot, turned[1], weights, weights, weights)


def token_products_kernel(count, *refs):
    low_refs, refs, grad_ref, turned_ref = (
        refs[:count], refs[count : 2 * count], refs[-2], refs[-1]
    )
    size = refs[0].shape[0]

    @pl.when(pl.program_id(0) == 0)
    def _():
        for place, ref in enumerate(low_refs):
            turned_ref[:, place * size : (place + 1) * size] = (
                ref[...].astype(F32).T.astype(BF16)
            )

    total = dot_nn(turned_ref[:, 0:size], refs[0][...])
    for place, ref in enumerate(refs[1:], 1):
        total = total + dot_nn(turned_ref[:, place * size : (place + 1) * size], ref[...])
    grad_ref[...] = total.astype(BF16)


def token_products(lows, parts, tile, first=0, tiles=None):
    size, model_width = lows[0].shape
    tiles = parts[0].shape[1] // tile if tiles is None else tiles
    columns = tiles * tile
    return pl.pallas_call(
        functools.partial(token_products_kernel, len(parts)),
        grid=(tiles,),
        in_specs=[whole_block(low) for low in lows]
        + [pl.BlockSpec((size, tile), lambda j: (0, first + j)) for unused in parts],
        out_specs=pl.BlockSpec((model_width, tile), lambda j: (0, j)),
        out_shape=jax.ShapeDtypeStruct((model_width, columns), BF16),
        scratch_shapes=[pltpu.VMEM((model_width, size * len(parts)), BF16)],
        compiler_params=pltpu.CompilerParams(vmem_limit_bytes=VMEM_BYTES),
        cost_estimate=pl.CostEstimate(
            flops=2 * model_width * size * columns,
            bytes_accessed=2 * model_width * columns,
            transcendentals=0,
        ),
        name="token_products",
    )(*lows, *parts)


ROWS = 256


def store_part(part_refs, values):
    block = pl.program_id(0)
    blocks = part_refs[0].shape[0] // ROWS
    for place, ref in enumerate(part_refs):

        @pl.when(block // blocks == place)
        def _(ref=ref):
            at = pl.multiple_of((block % blocks) * ROWS, ROWS)
            ref[pl.ds(at, ROWS), :] = values


def norm_kernel(rows_ref, gain_ref, *low_refs):
    rows = rows_ref[...].astype(F32)
    scale = lax.rsqrt(row_sum(rows * rows) * (1.0 / rows.shape[1]) + 1e-05)
    store_part(low_refs, (rows * scale * gain_ref[...]).astype(BF16))


def part_specs(parts):
    specs, starts, start = [], [], 0
    for part in parts:
        blocks = part.shape[0] // ROWS
        specs.append(
            pl.BlockSpec(
                (ROWS, part.shape[1]),
                lambda i, start=start, blocks=blocks: (jnp.clip(i - start, 0, blocks - 1), 0),
            )
        )
        starts.append(start)
        start += blocks
    return specs, starts


def gathered_rows(part_refs, starts, total_ref):
    block = pl.program_id(0)
    for refs, start, end in zip(part_refs, starts, starts[1:] + [1 << 30]):

        @pl.when((block >= start) & (block < end))
        def _(refs=refs):
            total = refs[0][...].astype(F32)
            for ref in refs[1:]:
                total = total + ref[...].astype(F32)
            total_ref[...] = total

    return total_ref[...]


def middle_kernel(starts, per_part, rows_ref, gain_ref, *refs):
    part_refs = refs[: len(starts) * per_part]
    middle_ref, second_ref, turned_ref, total_ref = refs[len(part_refs) :]
    grouped = [part_refs[at : at + per_part] for at in range(0, len(part_refs), per_part)]
    middle = rows_ref[...].astype(F32) + gathered_rows(grouped, starts, total_ref)
    scale = lax.rsqrt(row_sum(middle * middle) * (1.0 / middle.shape[1]) + 1e-05)
    second = middle * scale * gain_ref[...]
    middle_ref[...] = middle
    second_ref[...] = second.astype(BF16)
    turned_ref[...] = second.T.astype(BF16)


def norm_back(rows, gain, grad):
    width = rows.shape[1]
    scale = lax.rsqrt(row_sum(rows * rows) * (1.0 / width) + 1e-05)
    unit = rows * scale
    through = grad * gain
    grad_rows = scale * (through - unit * (row_sum(through * unit) * (1.0 / width)))
    return grad_rows, jnp.sum(grad * unit, axis=0, keepdims=True)


def add_rows(total_ref, row):
    @pl.when(pl.program_id(0) == 0)
    def _():
        total_ref[...] = jnp.zeros_like(total_ref)

    total_ref[...] += row


def second_back_kernel(
    back_ref, middle_ref, cot_ref, sum_ref, gain_ref, out_ref, grad_ref, gain_grad_ref, *low_refs
):
    middle = middle_ref[...]
    out_ref[...] = (middle + sum_ref[...]).astype(BF16)
    grad_rows, gain_grad = norm_back(middle, gain_ref[...], back_ref[...])
    add_rows(gain_grad_ref, gain_grad)
    grad_middle = cot_ref[...].astype(F32) + grad_rows
    grad_ref[...] = grad_middle
    store_part(low_refs, grad_middle.astype(BF16))


def first_back_kernel(starts, per_part, rows_ref, middle_grad_ref, gain_ref, *refs):
    part_refs = refs[: len(starts) * per_part]
    grad_ref, gain_grad_ref, total_ref = refs[len(part_refs) :]
    grouped = [part_refs[at : at + per_part] for at in range(0, len(part_refs), per_part)]
    grad = gathered_rows(grouped, starts, total_ref)
    grad_rows, gain_grad = norm_back(rows_ref[...].astype(F32), gain_ref[...], grad)
    add_rows(gain_grad_ref, gain_grad)
    grad_ref[...] = (middle_grad_ref[...] + grad_rows).astype(BF16)


def row_call(kernel, rows, operands, outs, scratch, name):
    width = rows[1]
    block = pl.BlockSpec((ROWS, width), lambda i: (i, 0))
    kinds = {
        "rows": (block, (rows[0], width)),
        "turned": (pl.BlockSpec((width, ROWS), lambda i: (0, i)), (width, rows[0])),
        "gain": (pl.BlockSpec((1, width), lambda i: (0, 0)), (1, width)),
    }
    part = min(PART, rows[0])
    kinds["part"] = (pl.BlockSpec((part, width), lambda i: (0, 0)), (part, width))
    return pl.pallas_call(
        kernel,
        grid=(rows[0] // ROWS,),
        in_specs=[block if spec is None else spec for unused, spec in operands],
        out_specs=[kinds[kind][0] for kind, unused in outs],
        out_shape=[jax.ShapeDtypeStruct(kinds[kind][1], dtype) for kind, dtype in outs],
        scratch_shapes=scratch,
        compiler_params=pltpu.CompilerParams(vmem_limit_bytes=VMEM_BYTES),
        name=name,
    )(*[array for array, unused in operands])


def norm_rows(rows, gain):
    gain = gain[None]
    return row_call(
        norm_kernel, rows.shape, [(rows, None), (gain, whole_block(gain))],
        [("part", BF16)] * max(1, rows.shape[0] // PART), [], "norm_rows"
    )


def middle_rows(rows, gain, parts):
    gain = gain[None]
    specs, starts = part_specs([terms[0] for terms in parts])
    operands = [(rows, None), (gain, whole_block(gain))]
    for terms, spec in zip(parts, specs):
        operands += [(term, spec) for term in terms]
    return row_call(
        functools.partial(middle_kernel, starts, len(parts[0])),
        rows.shape,
        operands,
        [("rows", F32), ("rows", BF16), ("turned", BF16)],
        [pltpu.VMEM((ROWS, rows.shape[1]), F32)],
        "middle_rows",
    )


def second_back(back, middle, cot, ffn_out, gain):
    gain = gain[None]
    return row_call(
        second_back_kernel,
        middle.shape,
        [(back, None), (middle, None), (cot, None), (ffn_out, None), (gain, whole_block(gain))],
        [("rows", BF16), ("rows", F32), ("gain", F32)]
        + [("part", BF16)] * max(1, middle.shape[0] // PART),
        [],
        "second_back",
    )


def first_back(rows, grad_middle, gain, parts):
    gain = gain[None]
    specs, starts = part_specs([terms[0] for terms in parts])
    operands = [(rows, None), (grad_middle, None), (gain, whole_block(gain))]
    for terms, spec in zip(parts, specs):
        operands += [(term, spec) for term in terms]
    return row_call(
        functools.partial(first_back_kernel, starts, len(parts[0])),
        rows.shape,
        operands,
        [("rows", BF16), ("gain", F32)],
        [pltpu.VMEM((ROWS, rows.shape[1]), F32)],
        "first_back",
    )


def share_kernel(kinds, own_ref, *refs):
    received, out_ref, share_ref = refs[:-2], refs[-2], refs[-1]
    rows, hidden = share_ref.shape[0], received[0].shape[1]
    for kind in range(kinds):
        at = slice(kind * rows, (kind + 1) * rows)
        total = own_ref[at, 0:hidden].astype(F32)
        for ref in received:
            total = total + ref[at, :].astype(F32)
        share_ref[:, kind * hidden : (kind + 1) * hidden] = total.astype(BF16)
    share_ref[:, kinds * hidden :] = out_ref[...]


def join_shares(own, received, out):
    hidden, rows = received[0].shape[1], out.shape[0]
    kinds = own.shape[0] // rows
    if hidden % 128:
        total = own[:, :hidden]
        for part in received:
            total = total + part
        return jnp.concatenate([*total.reshape(kinds, rows, hidden), out], axis=1)
    operands = (own, *received, out)
    shape = (rows, kinds * hidden + out.shape[1])
    return pl.pallas_call(
        functools.partial(share_kernel, kinds),
        grid=(1,),
        in_specs=[whole_block(array) for array in operands],
        out_specs=pl.BlockSpec(shape, lambda c: (0, 0)),
        out_shape=jax.ShapeDtypeStruct(shape, BF16),
        name="join_shares",
    )(*operands)


def spread_kernel(hidden, grads_ref, gate_up_ref, down_ref, out_ref, in_ref):
    grads = grads_ref[...]
    for kind in range(2):
        gate_up_ref[:, kind, :] = grads[:, kind * hidden : (kind + 1) * hidden].astype(F32)
    down_ref[...] = grads[:, 2 * hidden : 3 * hidden].astype(F32).T
    at = 3 * hidden
    out_ref[...] = grads[:, at : at + out_ref.shape[1]].astype(F32)
    at += out_ref.shape[1]
    heads, in_width = in_ref.shape[1:]
    for h in range(heads):
        in_ref[:, h, :] = grads[:, at + h * in_width : at + (h + 1) * in_width].astype(F32)


def spread_grads(grads, hidden, heads, in_width):
    model_width, columns = grads.shape
    out_width = columns - 3 * hidden - heads * in_width
    if hidden % 128:
        at = 3 * hidden + out_width
        wide = grads.astype(F32)
        return (
            wide[:, : 2 * hidden].reshape(model_width, 2, hidden),
            wide[:, 2 * hidden : 3 * hidden].T,
            wide[:, 3 * hidden : at],
            wide[:, at:].reshape(model_width, heads, in_width),
        )
    rows = 128

    def shape(*dims):
        return jax.ShapeDtypeStruct(dims, F32)

    return pl.pallas_call(
        functools.partial(spread_kernel, hidden),
        grid=(model_width // rows,),
        in_specs=[pl.BlockSpec((rows, columns), lambda c: (c, 0))],
        out_specs=[
            pl.BlockSpec((rows, 2, hidden), lambda c: (c, 0, 0)),
            pl.BlockSpec((hidden, rows), lambda c: (0, c)),
            pl.BlockSpec((rows, out_width), lambda c: (c, 0)),
            pl.BlockSpec((rows, heads, in_width), lambda c: (c, 0, 0)),
        ],
        out_shape=[
            shape(model_width, 2, hidden),
            shape(hidden, model_width),
            shape(model_width, out_width),
            shape(model_width, heads, in_width),
        ],
        compiler_params=pltpu.CompilerParams(vmem_limit_bytes=VMEM_BYTES),
        name="spread_grads",
    )(grads)


def after(array, other):
    return lax.optimization_barrier((array, other))[0]


def turn(array, axis, shift):
    size = lax.axis_size(axis)
    return lax.ppermute(array, axis, [((i + shift) % size, i) for i in range(size)])


def partner(array, axis, bit):
    return lax.ppermute(array, axis, [(i, i ^ bit) for i in range(lax.axis_size(axis))])


def is_power(size):
    return size & (size - 1) == 0


def sum_small(array, axis):
    size = lax.axis_size(axis)
    if not is_power(size):
        return lax.psum(array, axis)
    bit = 1
    while bit < size:
        array = array + partner(array, axis, bit)
        bit *= 2
    return array


def scatter_steps(array, meanwhile):
    size = lax.axis_size("dp")
    if not is_power(size):
        yield lax.psum_scatter(array, "dp", scatter_dimension=0, tiled=True)
        return
    index = lax.axis_index("dp")
    columns = array.shape[1]
    blocks = array.reshape(size, -1, columns)
    bit, step = 1, 0
    while bit < size:
        halves = blocks.reshape(-1, 2, blocks.shape[1], columns)
        mine = (index // bit) % 2
        keep = lax.dynamic_index_in_dim(halves, mine, 1, keepdims=False)
        send = lax.dynamic_index_in_dim(halves, 1 - mine, 1, keepdims=False)
        other = partner(send, "dp", bit)
        waits = meanwhile(step)
        if waits is not None:
            other = after(other, waits)
        blocks = keep + other
        bit, step = bit * 2, step + 1
        yield blocks if bit < size else blocks[0]


def shards(
    residual_in,
    mixer_gain,
    in_weight,
    rate_weight,
    conv_weight,
    decay_log,
    decay_bias,
    head_gain,
    out_weight,
    ffn_gain,
    gate_up,
    down_weight,
    segments,
    pad_mask,
    out_grad,
):
    rows_here, model_width = residual_in.shape
    heads_here, in_width = in_weight.shape[1:]
    hidden_here = gate_up.shape[2]
    members = lax.axis_size("tensor")
    share = lax.axis_size("dp")
    index = lax.axis_index("dp")
    pair = members == 2 and rows_here == SEQ
    value_dim = head_gain.shape[0]
    key_dim = (conv_weight.shape[2] - value_dim) // 2

    def sequences(own):
        if pair:
            return [own, [turn(part, "tensor", 1) for part in own]]
        whole = lax.all_gather(jnp.concatenate(own), "tensor", axis=0, tiled=True)
        return [
            [whole[at + by : at + by + PART] for by in range(0, SEQ, PART)]
            for at in range(0, whole.shape[0], SEQ)
        ]

    def token_parts(array):
        if pair:
            own = lax.axis_index("tensor")
            return [
                lax.dynamic_slice_in_dim(array, which * SEQ, SEQ) for which in (own, 1 - own)
            ]
        return [array[at : at + SEQ] for at in range(0, array.shape[0], SEQ)]

    def owner_parts(parts):
        if pair:
            return [[mine, other] for mine, other in zip(*parts)]
        return [
            [
                lax.psum_scatter(
                    jnp.concatenate([part for here in parts for part in here]).astype(BF16),
                    "tensor",
                    scatter_dimension=0,
                    tiled=True,
                )
            ]
        ]

    w_in = in_weight.reshape(model_width, heads_here * in_width)
    w_rate = jnp.pad(
        rate_weight.transpose(2, 1, 0), ((0, 0), (0, SLOTS - heads_here), (0, 0))
    ).reshape(2 * SLOTS, model_width)
    decay = jnp.pad(
        jnp.stack([-jnp.exp(decay_log), decay_bias], axis=1), ((0, SLOTS - heads_here), (0, 0))
    )
    w_out = out_weight.reshape(-1, model_width)
    conv_float = conv_weight.astype(F32)
    gain_row = head_gain[None]
    mixer_weights = (w_in, w_rate, w_out)
    normed = norm_rows(residual_in, mixer_gain)

    rows_share = model_width // share
    gate_up_piece = lax.dynamic_slice_in_dim(gate_up, index * rows_share, rows_share)
    piece = jnp.stack(
        [
            gate_up_piece[:, 0],
            gate_up_piece[:, 1],
            lax.dynamic_slice_in_dim(down_weight, index * rows_share, rows_share, axis=1).T,
        ]
    )
    pieces = [piece] + [
        after(turn(piece, "tensor", shift), (normed, w_in)) for shift in range(1, members)
    ]
    pieces = jnp.concatenate(
        [part[kind] for kind in range(3) for part in pieces], axis=1
    )
    weights = lax.all_gather(pieces, "dp", axis=0, tiled=True)
    first = sequences(normed)


    tables = [
        segment_tables(seg, mask, BLOCK)
        for seg, mask in zip(token_parts(segments), token_parts(pad_mask))
    ]
    local = len(first)
    count = SEQ // PART
    states = [jnp.zeros((heads_here, key_dim, value_dim), F32)] * local
    befores = [jnp.zeros((HALO, heads_here * in_width), BF16)] * local
    forward = [[None] * count for unused in range(local)]
    out_parts = [[None] * count for unused in range(local)]
    if pair:
        order = [(0, 0)] + [(1, p) for p in range(count)] + [(0, p) for p in range(1, count)]
    else:
        order = [(s, p) for p in range(count) for s in range(local)]
    done = None
    for place, (s, p) in enumerate(order):
        low_rows = first[s][p]
        if done is not None:
            low_rows = after(low_rows, done)
        if pair and place == len(order) - 1:
            low_rows = after(low_rows, arrived)
        table = tables[s][:, p * PART : (p + 1) * PART]
        travels = pair and s == 1
        part, proj, rates, cols, gated, *kept, states[s] = mixer_forward(
            low_rows, befores[s], table, mixer_weights, decay, conv_float, gain_row, states[s],
            BLOCK, BF16 if travels else F32,
        )
        forward[s][p] = (table, gated, (befores[s], proj, rates, cols, *kept))
        befores[s] = proj
        done = part
        out_parts[s][p] = part
        if travels:
            out_parts[s][p] = turn(part, "tensor", 1)
            if p < count - 1:
                arrived = out_parts[s][p]
    middle, second, second_turned = middle_rows(residual_in, ffn_gain, owner_parts(out_parts))
    ffn_out, grad_second, grads_ffn = feed_forward(
        second, second_turned, out_grad, weights, share
    )
    ffn_shares = lax.psum_scatter(
        grads_ffn.reshape(-1, grads_ffn.shape[-1]), "dp", scatter_dimension=0, tiled=True
    )
    layer_out, grad_middle, grad_ffn_gain, *grad_mix = second_back(
        grad_second, middle, out_grad, ffn_out, ffn_gain
    )
    cots = sequences(grad_mix)
    every = [(s, p) for s in range(local) for p in range(count)]
    grad_states = [jnp.zeros((heads_here, key_dim, value_dim), F32)] * local
    afters = [jnp.zeros((heads_here, HALO, conv_weight.shape[2]), F32)] * local
    first_parts = [[None] * count for unused in range(local)]
    proj_lows = [[None] * count for unused in range(local)]
    sums = 0.0
    done = None
    half = local * count // 2
    out_waits = {}
    grad_in = None
    for place, (s, p) in enumerate(reversed(order)):
        table, gated, kept = forward[s][p]
        cot = cots[s][p]
        if done is not None:
            cot = after(cot, done)
        if place == half:
            grad_out = token_products(
                [after(forward[s][p][1], done) for s, p in every],
                [cots[s][p] for s, p in every],
                model_width // 2,
            )
            out_steps = scatter_steps(grad_out, out_waits.get)
        if place >= half:
            share_out = next(out_steps)
            cot = after(cot, share_out)
        travels = pair and s == 1
        part, proj_low, grad_conv, grad_gain, grad_rate, grad_decay, grad_states[s], afters[s] = (
            mixer_backward(
                cot, first[s][p], table, mixer_weights, decay, conv_float, gain_row,
                kept, grad_states[s], afters[s], BLOCK, BF16 if travels else F32,
            )
        )
        proj_lows[s][p] = proj_low
        done = part
        first_parts[s][p] = turn(part, "tensor", 1) if travels else part
        out_waits[place - half + 1] = done
        grad_decay = jnp.sum(grad_decay.reshape(2, SLOTS, BLOCK), axis=2)
        sums = sums + jnp.concatenate(
            [
                grad_conv.reshape(-1),
                grad_gain[0],
                grad_decay[:, :heads_here].reshape(-1),
                grad_rate.reshape(2, SLOTS, model_width)[:, :heads_here].reshape(-1),
            ]
        )
    input_grad, grad_mixer_gain = first_back(
        residual_in, grad_middle, mixer_gain, owner_parts(first_parts)
    )
    proj_lows[0][0] = after(proj_lows[0][0], first_parts[-1])
    share_out = next(out_steps)
    proj_lows[0][0] = after(proj_lows[0][0], share_out)
    lows = [first[s][p] for s, p in every]
    proj_parts = [proj_lows[s][p] for s, p in every]
    columns = heads_here * in_width // 2
    tile = columns // 2 if columns % (2 * LANES) == 0 else columns
    grad_in_one = token_products(lows, proj_parts, tile, 0, columns // tile)
    out_waits[3] = grad_in_one
    for share_out in out_steps:
        pass
    waits_one, waits_two = {}, {}
    steps_one = scatter_steps(after(grad_in_one, share_out), waits_one.get)
    share_one = next(steps_one)
    proj_parts[0] = after(proj_parts[0], share_one)
    grad_in_two = token_products(lows, proj_parts, tile, columns // tile, columns // tile)
    small = jnp.concatenate([sums, grad_mixer_gain[0], grad_ffn_gain[0]])
    length = small.shape[0]
    small = jnp.pad(small, (0, -length % 1024)).reshape(-1, 1024)
    small = sum_small(small, "dp").reshape(-1)
    waits_one[1] = grad_in_two
    share_one = next(steps_one, share_one)
    steps_two = scatter_steps(after(grad_in_two, share_one), waits_two.get)
    share_two = next(steps_two)
    ffn_shares = after(ffn_shares, share_two)
    received = [
        turn(ffn_shares[:, shift * hidden_here : (shift + 1) * hidden_here], "tensor", -shift)
        for shift in range(1, members)
    ]
    share_early = join_shares(ffn_shares, received, share_out.reshape(rows_share, -1))
    waits_one[2] = share_two
    for step, share_one in enumerate(steps_one, 2):
        waits_two[step - 1] = [share_one, received] if step == 3 else share_one
        share_two = next(steps_two, share_two)
    waits_two[3] = share_early
    for share_two in steps_two:
        pass
    conv_size = conv_weight.size
    rate_size = rate_weight.size
    grad_conv = small[:conv_size].reshape(conv_weight.shape)
    at = conv_size + value_dim
    grad_log = small[at : at + heads_here]
    grad_bias = small[at + heads_here : at + 2 * heads_here]
    at += 2 * heads_here
    grad_rate = small[at : at + rate_size].reshape(2, heads_here, model_width).transpose(2, 1, 0)
    at += rate_size
    gains = jnp.concatenate([small[conv_size : conv_size + value_dim], small[at:length]])
    gains = sum_small(gains, "tensor")
    grad_head_gain = gains[:value_dim]
    grad_mixer_gain = gains[value_dim : value_dim + model_width]
    grad_ffn_gain = gains[value_dim + model_width :]

    grads = jnp.concatenate([share_early, share_one, share_two], axis=1)
    grads = lax.all_gather(grads, "dp", axis=0, tiled=True)
    grad_gate_up, grad_down, grad_out, grad_in = spread_grads(
        grads, hidden_here, heads_here, in_width
    )
    return (
        layer_out,
        input_grad,
        grad_mixer_gain,
        grad_in,
        grad_rate,
        grad_conv,
        grad_log,
        grad_bias,
        grad_head_gain,
        grad_out.reshape(out_weight.shape),
        grad_ffn_gain,
        grad_gate_up,
        grad_down,
    )


def solution(mesh):
    return jax.shard_map(
        shards,
        mesh=mesh,
        in_specs=(
            P(("dp", "tensor"), None),
            P(),
            P(None, "tensor", None),
            P(None, "tensor", None),
            P("tensor", None, None),
            P("tensor"),
            P("tensor"),
            P(),
            P("tensor", None, None),
            P(),
            P(None, None, "tensor"),
            P("tensor", None),
            P("dp"),
            P("dp"),
            P(("dp", "tensor"), None),
        ),
        out_specs=(
            P(("dp", "tensor"), None),
            P(("dp", "tensor"), None),
            P(),
            P(None, "tensor", None),
            P(None, "tensor", None),
            P("tensor", None, None),
            P("tensor"),
            P("tensor"),
            P(),
            P("tensor", None, None),
            P(),
            P(None, None, "tensor"),
            P("tensor", None),
        ),
        check_vma=False,
    )
```
